32 devices in a mesh: lon: 16 (over z, x, core), lat: 2 (over y).
Axes of the slice: x: 2, y: 2, z: 4, core: 2. Of those that a mesh axis runs over, the one named last changes fastest.
Arguments:
- increment: float32 [4, 512, 2048], P(None, 'lat', 'lon'), may hold values from -6 to 6
- kappa_x: float32 [4, 512, 2048], P(None, 'lat', 'lon'), may hold values from 0.02 to 0.2
- kappa_y: float32 [4, 512, 2048], P(None, 'lat', 'lon'), may hold values from 0.02 to 0.2
- metric_x: float32 [512, 2048], P('lat', 'lon'), may hold values from 0.5 to 1.5
- metric_y: float32 [512, 2048], P('lat', 'lon'), may hold values from 0.5 to 1.5
- cell_area: float32 [512, 2048], P('lat', 'lon'), may hold values from 1 to 2
- sea_mask: int32 [4, 512, 2048], P(None, 'lat', 'lon'), may hold values 0 or 1
- fold_partner: int32 [2048], P('lon'), may hold values from 0 to 2047, as said below
- norm_factor: float32 [4, 512, 2048], P(None, 'lat', 'lon'), may hold values from 0.5 to 36, as said below
Outputs:
- adjoint_out: float32 [4, 512, 2048], P(None, 'lat', 'lon')
The draws below stay inside these ranges and needn't reach their ends.
Inputs may be any that keep to these rules, and one draw needn't show every extreme that they name: fold_partner[i] = (c - i) mod 2048 for one c, so fold_partner[fold_partner[i]] = i. `norm_factor`: positive factors.
All inputs are finite; a program needn't handle non-finite values. No bound on the sum of `sea_mask` on one device may be relied on, other than what follows from the above.
Results may differ from the reference program's by a relative error of at most 0.00002.
Values sent between devices are 32-bit elements; how exact they have to be, the bound alone decides.
No kernel may reach another device: no remote copies, remote signals or barrier semaphores. Data moves between devices by JAX's collectives and lax.ppermute only.
A program may use at most 384 MiB of HBM per device.

```python
import math
import jax
import jax.numpy as jnp
from jax import lax

LEV = 4
STEPS = 6
NLAT = 512
NLON = 2048


def draw_fold_partner(key, part):
    center = jax.random.randint(key, (), 0, NLON, dtype=jnp.int32)
    return ((center - jnp.arange(NLON, dtype=jnp.int32)) % NLON).astype(jnp.int32)


def draw_norm_factor(key, part):
    base_key = jax.random.fold_in(key, 17)
    exponent = jax.random.uniform(base_key, (LEV, NLAT, NLON), jnp.float32, jnp.log(0.5), jnp.log(4.0))
    base = jnp.exp(exponent)
    rows = jnp.arange(NLAT, dtype=jnp.int32)
    distance = (NLAT - 1 - rows).astype(jnp.float32)
    rise = 1.0 + 8.0 * jnp.exp(-distance / 3.0)
    return (base * rise[None, :, None]).astype(jnp.float32)


def touch_ends(values, rng, smallest, high):
    longest = values.shape.index(max(values.shape))
    spots = []
    for shift in (0, 1):
        where = [jax.random.randint(jax.random.fold_in(rng, axis), (), 0, length) for axis, length in enumerate(values.shape)]
        where[longest] = (where[longest] + shift) % values.shape[longest]
        spots.append(tuple(where))
    return values.at[spots[0]].set(smallest).at[spots[1]].set(high)


def levels(own_key, extent, shards, low, largest):
    def one(dim, parts):
        steps = jax.random.uniform(jax.random.fold_in(jax.random.fold_in(own_key, 6), dim), (parts,), jnp.float32, low / len(shards), largest / len(shards))
        return jnp.repeat(jnp.exp(steps), extent[dim] // parts).reshape((-1,) + (1,) * (len(extent) - dim - 1))

    gain = one(*shards[0])
    for cut in shards[1:]:
        gain = gain * one(*cut)
    return gain


def noise(own_key, shape, width, reach, shards=(), kind=jnp.bfloat16):
    array = jax.random.normal(own_key, shape, jnp.float32) * width
    if len(shards) > 0:
        array = levels(own_key, shape, shards, -0.22, 0.18) * array
    return jnp.clip(array, min=-reach, max=reach).astype(kind)


def setup_inputs(seed: int = 0) -> dict:
    streams_of = jax.random.split(jax.random.key(seed), 10)
    increment = noise(streams_of[0], (LEV, NLAT, NLON), 1.0, 6.0, ((1, 2), (2, 16)), jnp.float32)
    kappa_x = jnp.clip(jnp.exp(math.log(0.2) - 2.3025851 * jax.random.uniform(streams_of[1], (LEV, NLAT, NLON), jnp.float32) ** levels(streams_of[1], (LEV, NLAT, NLON), ((1, 2), (2, 16)), -0.2, 0.2)), 0.02, 0.2)
    kappa_y = jnp.clip(jnp.exp(math.log(0.2) - 2.3025851 * jax.random.uniform(streams_of[2], (LEV, NLAT, NLON), jnp.float32) ** levels(streams_of[2], (LEV, NLAT, NLON), ((1, 2), (2, 16)), -0.2, 0.2)), 0.02, 0.2)
    metric_x = jnp.clip(1.0 + 0.1 * jax.random.normal(streams_of[3], (NLAT, NLON), jnp.float32), 0.5, 1.5)
    metric_y = jnp.clip(1.0 + 0.1 * jax.random.normal(streams_of[4], (NLAT, NLON), jnp.float32), 0.5, 1.5)
    cell_area = jnp.clip(1.0 + 1.0 * jax.random.uniform(streams_of[5], (NLAT, NLON), jnp.float32) ** levels(streams_of[5], (NLAT, NLON), ((0, 2), (1, 16)), -0.2, 0.2), 1.0, 2.0)
    sea_mask = touch_ends((jax.random.randint(streams_of[6], (LEV, NLAT, NLON), 0, 5) < 4).astype(jnp.int32), jax.random.fold_in(streams_of[6], 1), 0, 1)
    fold_partner = draw_fold_partner(jax.random.fold_in(streams_of[9], 71), 0)
    norm_factor = draw_norm_factor(jax.random.fold_in(streams_of[9], 71), 0)
    return dict(increment=increment, kappa_x=kappa_x, kappa_y=kappa_y, metric_x=metric_x, metric_y=metric_y, cell_area=cell_area, sea_mask=sea_mask, fold_partner=fold_partner, norm_factor=norm_factor)


def reference(increment, kappa_x, kappa_y, metric_x, metric_y, cell_area, sea_mask, fold_partner, norm_factor):
    def one_level(fields):
        field_now, kap_east, kap_north, mask_level, factor = fields
        sea_cells = mask_level.astype(jnp.float32)
        raw_x = kap_east * metric_x * sea_cells
        raw_y = kap_north * metric_y * sea_cells
        zero_row = jnp.zeros((1, sea_cells.shape[1]), jnp.float32)
        coef_east = raw_x * jnp.roll(sea_cells, -1, axis=1)
        coef_north = raw_y * jnp.concatenate([sea_cells[1:], zero_row], 0)
        top_y = raw_y[-1]
        top_sea = sea_cells[-1]
        coef_fold = 0.5 * (top_y * top_sea[fold_partner] + top_y[fold_partner] * top_sea)
        for step_index in range(STEPS):
            weighted = field_now / cell_area
            flux_e = coef_east * (jnp.roll(weighted, -1, axis=1) - weighted)
            north_w = jnp.concatenate([weighted[1:], zero_row], 0)
            flux_n = coef_north * (north_w - weighted)
            change = flux_e - jnp.roll(flux_e, 1, axis=1) + flux_n - jnp.concatenate([zero_row, flux_n[:-1]], 0)
            top_w = weighted[-1]
            change = change.at[-1].add(coef_fold * (top_w[fold_partner] - top_w))
            field_now = field_now + change
        return factor * field_now

    return lax.map(one_level, (increment, kappa_x, kappa_y, sea_mask, norm_factor))
```

```python
import functools

import jax
import jax.numpy as jnp
from jax import lax
from jax.experimental import pallas as pl
from jax.experimental.pallas import tpu as pltpu
from jax.sharding import PartitionSpec as P

STEPS = 6
LEV = 4
LANES = 128
SUB = 8
PAIR = LANES // 2
EDGES = LEV // 2
WEST = STEPS
EAST = 4 * STEPS
OWN = 2 * STEPS
PART = 4 * STEPS * EDGES
PLANES = 3 * LEV + 1
ALL = PLANES + 3 * EDGES + 1
VMEM_LIMIT = 60 * 1024 * 1024
F32 = jnp.float32


def lanes_of(shape):
    return lax.broadcasted_iota(jnp.int32, shape, 1)


def roll(x, shift):
    shift = shift % LANES
    return x if shift == 0 else pltpu.roll(x, shift, 1)


def half_lane(shape):
    return jnp.bitwise_and(lanes_of(shape), PAIR - 1)


def pair_up(low, high, shape):
    return jnp.where(lanes_of(shape) < PAIR, low, high)


def own_ends(low, high):
    shape = low.shape
    at = half_lane(shape)
    west = pair_up(roll(low, WEST), roll(high, PAIR + WEST), shape)
    east = pair_up(roll(low, EAST + OWN), roll(high, PAIR + EAST + OWN), shape)
    out = jnp.where((at >= WEST) & (at < WEST + OWN), west, 0.0)
    return jnp.where((at >= EAST) & (at < EAST + OWN), east, out)


def raw_fields(l, rows, inc, kx, ky, mx, my, mask, r):
    sea = mask[l, rows, :].astype(F32)
    return inc[l, rows, :] * r, kx[l, rows, :] * mx * sea, ky[l, rows, :] * my * sea


def pack_kernel(par, inc, kx, ky, mx, my, area, mask, edge_ref, m0_ref, m1_ref, acc0, acc1):
    half = inc.shape[1]
    chunk = 32
    even = par[0] == 0
    is_first = pl.program_id(0) == 0
    lane = lanes_of((chunk, LANES))
    for row in range(0, half, chunk):
        rows = pl.ds(row, chunk)
        r = 1.0 / area[rows, :]
        mxv, myv = mx[rows, :], my[rows, :]
        first = jnp.zeros((chunk, LANES), F32)
        last = jnp.zeros((chunk, LANES), F32)
        for l in range(LEV):
            fields = raw_fields(l, rows, inc, kx, ky, mxv, myv, mask, r) + (r,)
            for p, plane in enumerate(fields):
                at = PAIR * (l % 2) + 4 * STEPS * (l // 2) + STEPS * p
                here = (lane >= at) & (lane < at + STEPS)
                first = jnp.where(here, roll(plane, at), first)
                last = jnp.where(here, roll(plane, at + STEPS), last)
            store_edge(is_first, row, half, [(p * LEV + l, f) for p, f in enumerate(fields[:3])], edge_ref)
        store_edge(is_first, row, half, [(3 * LEV, r)], edge_ref)
        acc0[rows, :] = jnp.where(even, last, first)
        acc1[rows, :] = jnp.where(even, first, last)
    for acc, ref in ((acc0, m0_ref), (acc1, m1_ref)):
        turned = jnp.transpose(acc[...])
        ref[pl.ds(0, PART), :] = turned[:PART]
        ref[pl.ds(PART, PART), :] = turned[PAIR : PAIR + PART]


def store_edge(is_first, row, half, planes, edge_ref):
    side = 2 * SUB
    if row == 0:

        @pl.when(is_first)
        def _():
            for plane, value in planes:
                edge_ref[plane] = value[:side]

    if row == half - 2 * side:

        @pl.when(jnp.logical_not(is_first))
        def _():
            for plane, value in planes:
                edge_ref[plane] = value[side:]


def pack(par, inc, kx, ky, mx, my, area, mask):
    half = inc.shape[1] // 2
    cube = pl.BlockSpec((LEV, half, LANES), lambda i: (0, i, 0))
    flat = pl.BlockSpec((half, LANES), lambda i: (i, 0))
    msg = pl.BlockSpec((2 * PART, LANES), lambda i: (i, 0))
    msg_out = jax.ShapeDtypeStruct((4 * PART, LANES), F32)
    return pl.pallas_call(
        pack_kernel,
        grid=(2,),
        in_specs=[pl.BlockSpec(memory_space=pltpu.SMEM), cube, cube, cube, flat, flat, flat, cube],
        out_specs=[pl.BlockSpec((PLANES, 2 * SUB, LANES), lambda i: (0, 1 - i, 0)), msg, msg],
        out_shape=[jax.ShapeDtypeStruct((PLANES, 4 * SUB, LANES), F32), msg_out, msg_out],
        scratch_shapes=[pltpu.VMEM((half, LANES), F32), pltpu.VMEM((half, LANES), F32)],
        compiler_params=pltpu.CompilerParams(vmem_limit_bytes=VMEM_LIMIT),
        name="pack",
    )(par, inc, kx, ky, mx, my, area, mask)


def untranspose(msg_ref, half, buf):
    buf[pl.ds(0, PART), :] = msg_ref[pl.ds(2 * PART * half, PART), :]
    buf[pl.ds(PAIR, PART), :] = msg_ref[pl.ds(2 * PART * half + PART, PART), :]
    return jnp.transpose(buf[...])


def halo_half(par, g0, g1, half, buf):
    t0 = untranspose(g0, half, buf)
    t1 = untranspose(g1, half, buf)
    even = par[0] == 0
    return jnp.where(even, t1, t0), jnp.where(even, t0, t1)


def with_halo(own, west_t, east_t, e, p):
    at = half_lane(own.shape)
    slot = 4 * STEPS * e + STEPS * p
    out = jnp.where(at < WEST, roll(west_t, -slot), own)
    return jnp.where((at >= EAST + OWN) & (at < EAST + OWN + STEPS), roll(east_t, EAST + OWN - slot), out)


def edge_kernel(par, g0, g1, edge, hedge_ref, a_ref, b_ref, buf):
    rows = edge.shape[1]
    side = rows // 2
    lat_even = par[1] == 0
    buf[...] = jnp.zeros_like(buf)
    turned = []
    for half, lo in ((1, LANES - side), (0, 0)):
        wt, et = halo_half(par, g0, g1, half, buf)
        turned.append((wt[lo : lo + side], et[lo : lo + side]))
    west_t, east_t = [jnp.concatenate([turned[0][i], turned[1][i]], axis=0) for i in range(2)]
    for k in range(3 * EDGES + 1):
        p, e = divmod(k, EDGES)
        low, high = (edge[p * LEV + 2 * e], edge[p * LEV + 2 * e + 1]) if p < 3 else (edge[3 * LEV],) * 2
        value = with_halo(own_ends(low, high), west_t, east_t, e, p)
        hedge_ref[k] = value
        last, first = value[side - SUB : side], value[side : side + SUB]
        a_ref[PLANES + k] = jnp.where(lat_even, last, first)
        b_ref[PLANES + k] = jnp.where(lat_even, first, last)
    for p in range(PLANES):
        last, first = edge[p, side - SUB : side, :], edge[p, side : side + SUB, :]
        a_ref[p] = jnp.where(lat_even, last, first)
        b_ref[p] = jnp.where(lat_even, first, last)


def edge_messages(par, g0, g1, edge):
    vm = pl.BlockSpec(memory_space=pltpu.VMEM)
    msg = jax.ShapeDtypeStruct((ALL, SUB, LANES), F32)
    return pl.pallas_call(
        edge_kernel,
        in_specs=[pl.BlockSpec(memory_space=pltpu.SMEM), vm, vm, vm],
        out_specs=[vm, vm, vm],
        out_shape=[jax.ShapeDtypeStruct((ALL - PLANES, edge.shape[1], LANES), F32), msg, msg],
        scratch_shapes=[pltpu.VMEM((LANES, LANES), F32)],
        compiler_params=pltpu.CompilerParams(vmem_limit_bytes=VMEM_LIMIT),
        name="edge",
    )(par, g0, g1, edge)


def coefficients(x, y, r, c, at, n, coef, weights=None):
    rows, up, down = pl.ds(at, n), pl.ds(at + 1, n), pl.ds(at - 1, n)
    here = x[c, rows, :]
    xe, xw = roll(here, -1), roll(here, 1)
    sea = jnp.where(here > 0, 1.0, 0.0)
    yv, ys = y[c, rows, :], y[c, down, :]
    east = jnp.where(xe > 0, here, 0.0)
    west = xw * sea
    north = jnp.where(x[c, up, :] > 0, yv, 0.0)
    south = ys * sea
    if weights is not None:
        flip, n_own, n_far, s_own, s_far = weights
        sea_s = jnp.where(x[c, down, :] > 0, 1.0, 0.0)
        east = jnp.where(flip, xe * sea, east)
        west = jnp.where(flip, jnp.where(xw > 0, here, 0.0), west)
        north = n_own * north + n_far * (y[c, up, :] * sea)
        south = s_own * south + s_far * (yv * sea_s)
    east, west, north, south = r * east, r * west, r * north, r * south
    coef[0, c, rows, :] = east
    coef[1, c, rows, :] = west
    coef[2, c, rows, :] = north
    coef[3, c, rows, :] = south
    coef[4, c, rows, :] = 1.0 - ((east + west) + (north + south))


def advance(src, dst, coef, c, at, n):
    rows = pl.ds(at, n)
    here = src[c, rows, :]
    lon = coef[0, c, rows, :] * roll(here, -1) + coef[1, c, rows, :] * roll(here, 1)
    lat = coef[2, c, rows, :] * src[c, pl.ds(at + 1, n), :] + coef[3, c, rows, :] * src[c, pl.ds(at - 1, n), :]
    dst[c, rows, :] = coef[4, c, rows, :] * here + (lon + lat)


def run_steps(one, two, coef, count, lo, hi, n):
    def both(_, carry):
        for src, dst in ((one, two), (two, one)):
            for at in range(lo, hi, n):
                for c in range(count):
                    advance(src, dst, coef, c, at, n)
        return carry

    lax.fori_loop(0, STEPS // 2, both, 0)


def clear_pads(refs, count, lo, hi):
    zero = jnp.zeros((SUB, LANES), F32)
    for ref in refs:
        for c in range(count):
            ref[c, pl.ds(lo - SUB, SUB), :] = zero
            ref[c, pl.ds(hi, SUB), :] = zero


def inner_kernel(inc, kx, ky, mx, my, area, mask, out_ref, ends_ref, one, two, xb, yb, coef, kept):
    rows = inc.shape[1]
    n = 64
    lo, hi = SUB, SUB + rows
    odd = lax.rem(pl.program_id(0), 2) == 1
    clear_pads((one, two, xb, yb), 1, lo, hi)
    for at in range(0, rows, n):
        here, there = pl.ds(at, n), pl.ds(lo + at, n)
        r = 1.0 / area[here, :]
        w, rx, ry = raw_fields(0, here, inc, kx, ky, mx[here, :], my[here, :], mask, r)
        one[0, there, :] = w
        xb[0, there, :] = rx
        yb[0, there, :] = ry
        for k, value in enumerate((w, rx, ry, r)):

            @pl.when(jnp.logical_not(odd))
            def _():
                kept[k, here, :] = value

            @pl.when(odd)
            def _():
                ends_ref[0, k, here, :] = own_ends(kept[k, here, :], value)

    for at in range(lo, hi, n):
        coefficients(xb, yb, 1.0 / area[pl.ds(at - lo, n), :], 0, at, n, coef)
    run_steps(one, two, coef, 1, lo, hi, n)
    out_ref[0] = one[0, pl.ds(lo, rows), :]


def inner(inc, kx, ky, mx, my, area, mask):
    rows = inc.shape[1]
    cube = pl.BlockSpec((1, rows, LANES), lambda i: (i, 0, 0))
    flat = pl.BlockSpec((rows, LANES), lambda i: (0, 0))
    pad = rows + 2 * SUB
    cells = pltpu.VMEM((1, pad, LANES), F32)
    return pl.pallas_call(
        inner_kernel,
        grid=(LEV,),
        in_specs=[cube, cube, cube, flat, flat, flat, cube],
        out_specs=[cube, pl.BlockSpec((1, 4, rows, LANES), lambda i: (i // 2, 0, 0, 0))],
        out_shape=[jax.ShapeDtypeStruct(inc.shape, F32), jax.ShapeDtypeStruct((EDGES, 4, rows, LANES), F32)],
        scratch_shapes=[
            cells,
            cells,
            cells,
            cells,
            pltpu.VMEM((5, 1, pad, LANES), F32),
            pltpu.VMEM((4, rows, LANES), F32),
        ],
        compiler_params=pltpu.CompilerParams(vmem_limit_bytes=VMEM_LIMIT),
        cost_estimate=pl.CostEstimate(flops=12_000_000, bytes_accessed=6_000_000, transcendentals=0),
        name="inner",
    )(inc, kx, ky, mx, my, area, mask)


def merge(own, ends, l):
    lane = lanes_of(own.shape)
    at = PAIR * (l % 2)
    out = jnp.where(lane < STEPS, roll(ends, -(at + WEST)), own)
    return jnp.where(lane >= LANES - STEPS, roll(ends, -(at + EAST + OWN)), out)


def ends_kernel(par, ends, g0, g1, mid, norm, area, out_ref, scale_ref, one, two, xb, yb, rb, coef, buf):
    rows = mid.shape[1]
    n = 64
    lo, hi = SUB, SUB + rows
    buf[...] = jnp.zeros_like(buf)
    clear_pads((one, two, xb, yb), EDGES, lo, hi)
    for half in range(2):
        wt, et = halo_half(par, g0, g1, half, buf)
        here, there = pl.ds(half * LANES, LANES), pl.ds(lo + half * LANES, LANES)
        for e in range(EDGES):
            one[e, there, :] = with_halo(ends[e, 0, here, :], wt, et, e, 0)
            xb[e, there, :] = with_halo(ends[e, 1, here, :], wt, et, e, 1)
            yb[e, there, :] = with_halo(ends[e, 2, here, :], wt, et, e, 2)
        rb[there, :] = with_halo(ends[0, 3, here, :], wt, et, 0, 3)
    for at in range(lo, hi, n):
        for e in range(EDGES):
            coefficients(xb, yb, rb[pl.ds(at, n), :], e, at, n, coef)
    run_steps(one, two, coef, EDGES, lo, hi, n)
    for l in range(LEV):
        scale = norm[l] * area[...]
        out_ref[l] = scale * merge(mid[l], one[l // 2, pl.ds(lo, rows), :], l)
        scale_ref[l, :SUB, :] = scale[rows - SUB :]
        scale_ref[l, SUB:, :] = scale[:SUB]


def lon_ends(par, ends, g0, g1, mid, norm, area):
    rows = mid.shape[1]
    vm = pl.BlockSpec(memory_space=pltpu.VMEM)
    pad = rows + 2 * SUB
    cells = pltpu.VMEM((EDGES, pad, LANES), F32)
    return pl.pallas_call(
        ends_kernel,
        in_specs=[pl.BlockSpec(memory_space=pltpu.SMEM)] + [vm] * 6,
        out_specs=[vm, vm],
        out_shape=[jax.ShapeDtypeStruct(mid.shape, F32), jax.ShapeDtypeStruct((LEV, 2 * SUB, LANES), F32)],
        scratch_shapes=[
            cells,
            cells,
            cells,
            cells,
            pltpu.VMEM((pad, LANES), F32),
            pltpu.VMEM((5, EDGES, pad, LANES), F32),
            pltpu.VMEM((LANES, LANES), F32),
        ],
        compiler_params=pltpu.CompilerParams(vmem_limit_bytes=VMEM_LIMIT),
        cost_estimate=pl.CostEstimate(flops=8_000_000, bytes_accessed=4_000_000, transcendentals=0),
        name="ends",
    )(par, ends, g0, g1, mid, norm, area)


def gather(x, idx):
    return jnp.take_along_axis(x, idx, axis=1)


def mirrored(b1, b2, first):
    shape = (SUB, LANES)
    lane, at = lanes_of(shape), half_lane(shape)
    flip = SUB - 1 - lax.broadcasted_iota(jnp.int32, shape, 0)
    own_j = first - lane
    own_i = jnp.bitwise_and(own_j, LANES - 1)
    end_j = first - jnp.where(at < EAST, at - WEST, at - EAST + LANES - OWN)
    end_i = jnp.bitwise_and(end_j, LANES - 1)

    def rows(x):
        return jnp.take_along_axis(x, flip, axis=0)

    def pick(j, idx, beyond1, one, two, beyond2):
        out = jnp.where(j >= 0, gather(one, idx), gather(two, idx))
        out = jnp.where(j >= LANES, gather(beyond1, idx), out)
        return jnp.where(j < -LANES, gather(beyond2, idx), out)

    out = {}
    for k in range(3 * EDGES + 1):
        p, e = divmod(k, EDGES)
        ends1, ends2 = b1[PLANES + k], b2[PLANES + k]
        both = []
        for q in range(2):
            plane = p * LEV + 2 * e + q if p < 3 else 3 * LEV
            one, two = b1[plane], b2[plane]
            if p < 3 or q == 0:
                out[plane] = rows(jnp.where(own_j >= 0, gather(one, own_i), gather(two, own_i)))
            beyond1 = roll(ends1, -(PAIR * q + EAST + OWN))
            beyond2 = roll(ends2, -(PAIR * q + WEST))
            both.append(pick(end_j, end_i, beyond1, one, two, beyond2))
        out[PLANES + k] = rows(pair_up(both[0], both[1], shape))
    return out


def band_kernel(par, edge, hedge, ga, gb, gc, scale, old, out_ref, one, two, xb, yb, rb, coef, res, sem):
    del old
    side = edge.shape[1] // 2
    count = LEV + EDGES
    lat_even = par[1] == 0
    is_top = par[2] == 1
    lo = SUB
    north, south, own = lo + side, lo + side + SUB, lo + side + 2 * SUB
    hi = own + side
    clear_pads((one, two, xb, yb), count, lo, hi)

    def place(plane):
        if plane < 3 * LEV:
            return (one, xb, yb)[plane // LEV].at[plane % LEV]
        if plane == 3 * LEV:
            return rb.at[0]
        p, e = divmod(plane - PLANES, EDGES)
        return rb.at[1] if p == 3 else (one, xb, yb)[p].at[LEV + e]

    for plane in range(ALL):
        ref = place(plane)
        mine = edge.at[plane] if plane < PLANES else hedge.at[plane - PLANES]
        ref[pl.ds(lo, side), :] = mine[:side, :]
        ref[pl.ds(own, side), :] = mine[side:, :]
        ref[pl.ds(south, SUB), :] = jnp.where(lat_even, gb[plane], ga[plane])

    @pl.when(is_top)
    def _():
        for plane, value in mirrored(gb, gc, par[3]).items():
            place(plane)[pl.ds(north, SUB), :] = value

    @pl.when(jnp.logical_not(is_top))
    def _():
        for plane in range(ALL):
            place(plane)[pl.ds(north, SUB), :] = jnp.where(lat_even, ga[plane], gb[plane])

    n = hi - lo
    row = lo + lax.broadcasted_iota(jnp.int32, (n, LANES), 0)
    fold = is_top & (row >= north) & (row < south)
    n_far = jnp.where(is_top & (row == north - 1), 0.5, jnp.where(fold, 1.0, 0.0))
    s_far = jnp.where(is_top & (row == north), 0.5, jnp.where(fold, 1.0, 0.0))
    weights = (fold, 1.0 - n_far, n_far, 1.0 - s_far, s_far)
    for c in range(count):
        coefficients(xb, yb, rb[c // LEV, pl.ds(lo, n), :], c, lo, n, coef, weights)
    run_steps(one, two, coef, count, lo, hi, n)
    for l in range(LEV):
        for i, at in enumerate((north - SUB, own)):
            rows = pl.ds(at, SUB)
            value = merge(one[l, rows, :], one[LEV + l // 2, rows, :], l)
            res[i, l] = scale[l, i * SUB : (i + 1) * SUB, :] * value
    rows = out_ref.shape[1]
    copies = [
        pltpu.make_async_copy(res.at[0], out_ref.at[:, pl.ds(rows - SUB, SUB), :], sem.at[0]),
        pltpu.make_async_copy(res.at[1], out_ref.at[:, pl.ds(0, SUB), :], sem.at[1]),
    ]
    for copy in copies:
        copy.start()
    for copy in copies:
        copy.wait()


def band(par, edge, hedge, ga, gb, gc, scale, out):
    vm = pl.BlockSpec(memory_space=pltpu.VMEM)
    anywhere = pl.BlockSpec(memory_space=pl.ANY)
    pad = edge.shape[1] + 4 * SUB
    cells = pltpu.VMEM((LEV + EDGES, pad, LANES), F32)
    return pl.pallas_call(
        band_kernel,
        in_specs=[pl.BlockSpec(memory_space=pltpu.SMEM)] + [vm] * 6 + [anywhere],
        out_specs=anywhere,
        out_shape=jax.ShapeDtypeStruct(out.shape, F32),
        input_output_aliases={7: 0},
        scratch_shapes=[
            cells,
            cells,
            cells,
            cells,
            pltpu.VMEM((2, pad, LANES), F32),
            pltpu.VMEM((5, LEV + EDGES, pad, LANES), F32),
            pltpu.VMEM((2, LEV, SUB, LANES), F32),
            pltpu.SemaphoreType.DMA((2,)),
        ],
        compiler_params=pltpu.CompilerParams(vmem_limit_bytes=VMEM_LIMIT),
        name="band",
    )(par, edge, hedge, ga, gb, gc, scale, out)


def table(axes, sizes, send):
    place = {axis: i for i, axis in enumerate(axes)}

    def flat(lon, lat):
        spot = {"lon": lon, "lat": lat}
        index = 0
        for axis in axes:
            index = index * sizes[axis] + spot[axis]
        return index

    pairs = []
    for lon in range(sizes["lon"]):
        for lat in range(sizes["lat"]):
            to = send(lon, lat)
            if to is not None:
                pairs.append((flat(lon, lat), flat(to[0] % sizes["lon"], to[1])))
    return pairs


def per_device(axes, sizes, inc, kx, ky, mx, my, area, mask, fold_partner, norm):
    n_lon, n_lat = sizes["lon"], sizes["lat"]
    cols = inc.shape[2]
    lon, lat = lax.axis_index("lon"), lax.axis_index("lat")
    center = lax.rem(fold_partner[0] + lon * cols, n_lon * cols)
    fold_block = center // cols
    par = jnp.stack(
        [lax.rem(lon, 2), lax.rem(lat, 2), jnp.where(lat == n_lat - 1, 1, 0), lax.rem(center, cols)]
    ).astype(jnp.int32)

    def permute(x, send):
        return lax.ppermute(x, axes, table(axes, sizes, send))

    edge, m0, m1 = pack(par, inc, kx, ky, mx, my, area, mask)
    g0 = permute(m0, lambda o, a: (o + 1 - 2 * (o % 2), a))
    g1 = permute(m1, lambda o, a: (o - 1 + 2 * (o % 2), a))
    mid, ends = inner(inc, kx, ky, mx, my, area, mask)
    hedge, ma, mb = edge_messages(par, g0, g1, edge)
    ga = permute(ma, lambda o, a: (o, a + 1 - 2 * (a % 2)))

    def fold_exchange(block):
        def first(o, a):
            if a == n_lat - 1:
                return block - o, a
            to = a - 1 + 2 * (a % 2)
            return (o, to) if 0 <= to < n_lat else None

        def second(o, a):
            return (block - 1 - o, a) if a == n_lat - 1 else None

        def exchange(x, *others):
            return (permute(x, first), permute(x, second)) + tuple(lon_ends(par, *others))

        return exchange

    branches = [fold_exchange(block) for block in range(n_lon)]
    gb, gc, out, scale = lax.switch(fold_block, branches, mb, ends, g0, g1, mid, norm, area)
    return band(par, edge, hedge, ga, gb, gc, scale, out)


def solution(mesh):
    axes = tuple(mesh.axis_names)
    sizes = dict(mesh.shape)
    cube, flat = P(None, "lat", "lon"), P("lat", "lon")
    return jax.shard_map(
        functools.partial(per_device, axes, sizes),
        mesh=mesh,
        in_specs=(cube, cube, cube, flat, flat, flat, cube, P("lon"), cube),
        out_specs=cube,
        check_vma=False,
    )
```

```python
import functools

import jax
import jax.numpy as jnp
from jax import lax
from jax.experimental import pallas as pl
from jax.experimental.pallas import tpu as pltpu
from jax.sharding import PartitionSpec as P

STEPS = 6
LEV = 4
LANES = 128
SUB = 8
PAIR = LANES // 2
EDGES = LEV // 2
WEST = STEPS
EAST = 4 * STEPS
OWN = 2 * STEPS
PART = 4 * STEPS * EDGES
PLANES = 3 * LEV + 1
ENDS = 3 * EDGES + 1
ALL = PLANES + ENDS
FOLD = 2 * PLANES + ENDS
LEAD_FLOPS = 10_000_000_000
VMEM_LIMIT = 24 * 1024 * 1024
F32 = jnp.float32


def is_even(axis):
    return lax.rem(lax.axis_index(axis), 2) == 0


def lanes_of(shape):
    return lax.broadcasted_iota(jnp.int32, shape, 1)


def roll(x, shift):
    shift = shift % LANES
    return x if shift == 0 else pltpu.roll(x, shift, 1)


def half_lane(shape):
    return jnp.bitwise_and(lanes_of(shape), PAIR - 1)


def pair_up(low, high, shape):
    return jnp.where(lanes_of(shape) < PAIR, low, high)


def own_ends(low, high):
    shape = low.shape
    at = half_lane(shape)
    west = pair_up(roll(low, WEST), roll(high, PAIR + WEST), shape)
    east = pair_up(roll(low, EAST + OWN), roll(high, PAIR + EAST + OWN), shape)
    out = jnp.where((at >= WEST) & (at < WEST + OWN), west, 0.0)
    return jnp.where((at >= EAST) & (at < EAST + OWN), east, out)


def lead_kernel(out_ref):
    out_ref[...] = jnp.zeros_like(out_ref)


def lead():
    return pl.pallas_call(
        lead_kernel,
        out_specs=pl.BlockSpec(memory_space=pltpu.VMEM),
        out_shape=jax.ShapeDtypeStruct((SUB, LANES), F32),
        compiler_params=pltpu.CompilerParams(vmem_limit_bytes=1024 * 1024),
        cost_estimate=pl.CostEstimate(flops=LEAD_FLOPS, bytes_accessed=32, transcendentals=0),
        name="lead",
    )()


def raw_fields(l, rows, inc, kx, ky, mx, my, mask, r):
    sea = mask[l, rows, :].astype(F32)
    return inc[l, rows, :] * r, kx[l, rows, :] * mx * sea, ky[l, rows, :] * my * sea


def pack_kernel(start, inc, kx, ky, mx, my, area, mask, edge_ref, m0_ref, m1_ref, acc_first, acc_last):
    del start
    rows = inc.shape[1]
    columns = m1_ref.shape[0]
    chunk = 32
    side = 2 * SUB
    even = is_even("lon")
    lane = lanes_of((chunk, LANES))
    for at in range(0, rows, chunk):
        here = pl.ds(at, chunk)
        r = 1.0 / area[here, :]
        mxv, myv = mx[here, :], my[here, :]
        first = jnp.zeros((chunk, LANES), F32)
        last = jnp.zeros((chunk, LANES), F32)
        planes = [None] * PLANES
        planes[3 * LEV] = r
        for l in range(LEV):
            fields = raw_fields(l, here, inc, kx, ky, mxv, myv, mask, r) + (r,)
            planes[l : 3 * LEV : LEV] = fields[:3]
            for p, plane in enumerate(fields):
                lane_at = PAIR * (l % 2) + 4 * STEPS * (l // 2) + STEPS * (p + 1)
                turned = roll(plane, lane_at)
                first = jnp.where((lane >= lane_at) & (lane < lane_at + STEPS), turned, first)
                last = jnp.where((lane >= lane_at - STEPS) & (lane < lane_at), turned, last)
        acc_first[here, :] = first
        acc_last[here, :] = last
        if at == 0:
            for p in range(PLANES):
                edge_ref[p, side:, :] = planes[p][:side]
        if at == rows - chunk:
            for p in range(PLANES):
                edge_ref[p, :side, :] = planes[p][chunk - side :]
                m0_ref[pl.ds(columns + SUB * p, SUB), :] = planes[p][chunk - SUB :]
    for i in range(rows // LANES):
        first = jnp.transpose(acc_first[pl.ds(i * LANES, LANES), :])
        last = jnp.transpose(acc_last[pl.ds(i * LANES, LANES), :])
        for q in range(2):
            to = pl.ds((2 * i + q) * PART, PART)
            one = first[PAIR * q + STEPS : PAIR * q + STEPS + PART]
            two = last[PAIR * q : PAIR * q + PART]
            m0_ref[to, :] = jnp.where(even, two, one)
            m1_ref[to, :] = jnp.where(even, one, two)


def pack(start, *fields):
    shape = fields[0].shape
    vm = pl.BlockSpec(memory_space=pltpu.VMEM)
    columns = shape[1] // LANES * 2 * PART
    acc = pltpu.VMEM(shape[1:], F32)
    return pl.pallas_call(
        pack_kernel,
        in_specs=[pl.BlockSpec(memory_space=pl.ANY)] + [vm] * 7,
        out_specs=[vm, vm, vm],
        out_shape=[jax.ShapeDtypeStruct((PLANES, 4 * SUB, LANES), F32)]
        + [jax.ShapeDtypeStruct((n, LANES), F32) for n in (columns + PLANES * SUB, columns)],
        scratch_shapes=[acc, acc],
        compiler_params=pltpu.CompilerParams(vmem_limit_bytes=VMEM_LIMIT),
        name="pack",
    )(start, *fields)


def untranspose(msg_ref, half, buf):
    buf[pl.ds(0, PART), :] = msg_ref[pl.ds(2 * PART * half, PART), :]
    buf[pl.ds(PAIR, PART), :] = msg_ref[pl.ds(2 * PART * half + PART, PART), :]
    return jnp.transpose(buf[...])


def halo_half(g0, g1, half, buf):
    t0 = untranspose(g0, half, buf)
    t1 = untranspose(g1, half, buf)
    even = is_even("lon")
    return jnp.where(even, t1, t0), jnp.where(even, t0, t1)


def with_halo(own, west_t, east_t, e, p):
    at = half_lane(own.shape)
    slot = 4 * STEPS * e + STEPS * p
    out = jnp.where(at < WEST, roll(west_t, -slot), own)
    return jnp.where((at >= EAST + OWN) & (at < EAST + OWN + STEPS), roll(east_t, EAST + OWN - slot), out)


def edge_kernel(g0, g1, edge, hedge_ref, fold_ref, *lat_refs):
    rows = edge.shape[1]
    side = rows // 2
    columns = g1.shape[0]
    even = is_even("lon")
    buf = lat_refs[-1]
    buf[...] = jnp.zeros_like(buf)
    turned = []
    for half, lo in ((1, LANES - side), (0, 0)):
        wt, et = halo_half(g0, g1, half, buf)
        turned.append((wt[lo : lo + side], et[lo : lo + side]))
    west_t, east_t = [jnp.concatenate([turned[0][i], turned[1][i]], axis=0) for i in range(2)]

    def to_lat(k, last, first):
        for ref, even_sends, odd_sends in zip(lat_refs[:-1], (last, first), (first, last)):
            ref[k] = jnp.where(is_even("lat"), even_sends, odd_sends)

    for k in range(ENDS):
        p, e = divmod(k, EDGES)
        low, high = (edge[p * LEV + 2 * e], edge[p * LEV + 2 * e + 1]) if p < 3 else (edge[3 * LEV],) * 2
        value = with_halo(own_ends(low, high), west_t, east_t, e, p)
        hedge_ref[k] = value
        fold_ref[2 * PLANES + k] = value[side - SUB : side]
        to_lat(PLANES + k, value[side - SUB : side], value[side : side + SUB])
    for p in range(PLANES):
        last, first = edge[p, side - SUB : side, :], edge[p, side : side + SUB, :]
        other = g0[pl.ds(columns + SUB * p, SUB), :]
        fold_ref[p] = jnp.where(even, last, other)
        fold_ref[PLANES + p] = jnp.where(even, other, last)
        to_lat(p, last, first)


def edge_messages(g0, g1, edge, lats):
    vm = pl.BlockSpec(memory_space=pltpu.VMEM)
    shapes = [(ENDS, edge.shape[1]), (FOLD, SUB)] + [(ALL, SUB)] * lats
    return pl.pallas_call(
        edge_kernel,
        in_specs=[vm, vm, vm],
        out_specs=[vm] * len(shapes),
        out_shape=[jax.ShapeDtypeStruct(shape + (LANES,), F32) for shape in shapes],
        scratch_shapes=[pltpu.VMEM((LANES, LANES), F32)],
        compiler_params=pltpu.CompilerParams(vmem_limit_bytes=VMEM_LIMIT),
        name="edge",
    )(g0, g1, edge)


def coefficients(x, y, r, c, at, n, coef, weights=None):
    rows, up, down = pl.ds(at, n), pl.ds(at + 1, n), pl.ds(at - 1, n)
    here = x[c, rows, :]
    xe, xw = roll(here, -1), roll(here, 1)
    sea = jnp.where(here > 0, 1.0, 0.0)
    yv, ys = y[c, rows, :], y[c, down, :]
    east = jnp.where(xe > 0, here, 0.0)
    west = xw * sea
    north = jnp.where(x[c, up, :] > 0, yv, 0.0)
    south = ys * sea
    if weights is not None:
        flip, n_own, n_far, s_own, s_far = weights
        sea_s = jnp.where(x[c, down, :] > 0, 1.0, 0.0)
        east = jnp.where(flip, xe * sea, east)
        west = jnp.where(flip, jnp.where(xw > 0, here, 0.0), west)
        north = n_own * north + n_far * (y[c, up, :] * sea)
        south = s_own * south + s_far * (yv * sea_s)
    east, west, north, south = r * east, r * west, r * north, r * south
    coef[0, c, rows, :] = east
    coef[1, c, rows, :] = west
    coef[2, c, rows, :] = north
    coef[3, c, rows, :] = south
    coef[4, c, rows, :] = 1.0 - ((east + west) + (north + south))


def advance(src, dst, coef, c, at, n):
    rows = pl.ds(at, n)
    here = src[c, rows, :]
    lon = coef[0, c, rows, :] * roll(here, -1) + coef[1, c, rows, :] * roll(here, 1)
    lat = coef[2, c, rows, :] * src[c, pl.ds(at + 1, n), :] + coef[3, c, rows, :] * src[c, pl.ds(at - 1, n), :]
    dst[c, rows, :] = coef[4, c, rows, :] * here + (lon + lat)


def run_steps(one, two, coef, count, lo, hi, n):
    def both(_, carry):
        for src, dst in ((one, two), (two, one)):
            for at in range(lo, hi, n):
                for c in range(count):
                    advance(src, dst, coef, c, at, n)
        return carry

    lax.fori_loop(0, STEPS // 2, both, 0)


def clear_pads(refs, count, lo, hi):
    zero = jnp.zeros((SUB, LANES), F32)
    for ref in refs:
        for c in range(count):
            ref[c, pl.ds(lo - SUB, SUB), :] = zero
            ref[c, pl.ds(hi, SUB), :] = zero


def inner_kernel(partner, inc, kx, ky, mx, my, area, mask, out_ref, ends_ref, chip_ref, mirror_ref, one, two, xb, yb, rb, coef):
    rows = inc.shape[1]
    n = 16
    lo, hi = SUB, SUB + rows
    columns = lax.axis_size("lon") * LANES
    lane = lanes_of((1, LANES))
    head = jnp.sum(jnp.where(lane == 0, partner[...].reshape(1, LANES), 0))
    center = lax.rem(head + lax.axis_index("lon") * LANES, columns)
    chip_ref[0] = center // (2 * LANES)
    mirror_ref[0] = lax.rem(center, 2 * LANES) + (2 - lax.rem(lax.axis_index("lon"), 2)) * LANES
    clear_pads((one, two, xb, yb), LEV, lo, hi)
    for at in range(0, rows, n):
        here, there = pl.ds(at, n), pl.ds(lo + at, n)
        r = 1.0 / area[here, :]
        rb[here, :] = r
        mxv, myv = mx[here, :], my[here, :]
        fields = [raw_fields(l, here, inc, kx, ky, mxv, myv, mask, r) for l in range(LEV)]
        for l in range(LEV):
            one[l, there, :], xb[l, there, :], yb[l, there, :] = fields[l]
        for e in range(EDGES):
            for p in range(3):
                ends_ref[p * EDGES + e, here, :] = own_ends(fields[2 * e][p], fields[2 * e + 1][p])
        ends_ref[3 * EDGES, here, :] = own_ends(r, r)
    for at in range(lo, hi, n):
        for l in range(LEV):
            coefficients(xb, yb, rb[pl.ds(at - lo, n), :], l, at, n, coef)
    run_steps(one, two, coef, LEV, lo, hi, n)
    for l in range(LEV):
        out_ref[l] = one[l, pl.ds(lo, rows), :]


def inner(partner, *fields):
    shape = fields[0].shape
    rows = shape[1]
    vm, sm = pl.BlockSpec(memory_space=pltpu.VMEM), pl.BlockSpec(memory_space=pltpu.SMEM)
    pad = rows + 2 * SUB
    cells = pltpu.VMEM((LEV, pad, LANES), F32)
    return pl.pallas_call(
        inner_kernel,
        in_specs=[vm] * 8,
        out_specs=[vm, vm, sm, sm],
        out_shape=[
            jax.ShapeDtypeStruct(shape, F32),
            jax.ShapeDtypeStruct((ENDS, rows, LANES), F32),
            jax.ShapeDtypeStruct((1,), jnp.int32),
            jax.ShapeDtypeStruct((1,), jnp.int32),
        ],
        scratch_shapes=[
            cells,
            cells,
            cells,
            cells,
            pltpu.VMEM((rows, LANES), F32),
            pltpu.VMEM((5, LEV, pad, LANES), F32),
        ],
        compiler_params=pltpu.CompilerParams(vmem_limit_bytes=VMEM_LIMIT),
        cost_estimate=pl.CostEstimate(flops=12_000_000, bytes_accessed=6_000_000, transcendentals=0),
        name="inner",
    )(partner, *fields)


def merge(own, ends, l):
    lane = lanes_of(own.shape)
    at = PAIR * (l % 2)
    out = jnp.where(lane < STEPS, roll(ends, -(at + WEST)), own)
    return jnp.where(lane >= LANES - STEPS, roll(ends, -(at + EAST + OWN)), out)


def ends_kernel(ends, g0, g1, mid, norm, area, out_ref, scale_ref, one, two, xb, yb, rb, coef, buf):
    rows = mid.shape[1]
    n = 16
    lo, hi = SUB, SUB + rows
    buf[...] = jnp.zeros_like(buf)
    clear_pads((one, two, xb, yb), EDGES, lo, hi)
    for half in range(2):
        wt, et = halo_half(g0, g1, half, buf)
        here, there = pl.ds(half * LANES, LANES), pl.ds(lo + half * LANES, LANES)
        for e in range(EDGES):
            one[e, there, :] = with_halo(ends[e, here, :], wt, et, e, 0)
            xb[e, there, :] = with_halo(ends[EDGES + e, here, :], wt, et, e, 1)
            yb[e, there, :] = with_halo(ends[2 * EDGES + e, here, :], wt, et, e, 2)
        rb[there, :] = with_halo(ends[3 * EDGES, here, :], wt, et, 0, 3)
    for at in range(lo, hi, n):
        for e in range(EDGES):
            coefficients(xb, yb, rb[pl.ds(at, n), :], e, at, n, coef)
    run_steps(one, two, coef, EDGES, lo, hi, n)
    for l in range(LEV):
        scale = norm[l] * area[...]
        out_ref[l] = scale * merge(mid[l], one[l // 2, pl.ds(lo, rows), :], l)
        scale_ref[l, :SUB, :] = scale[rows - SUB :]
        scale_ref[l, SUB:, :] = scale[:SUB]


def lon_ends(ends, g0, g1, mid, norm, area):
    rows = mid.shape[1]
    vm = pl.BlockSpec(memory_space=pltpu.VMEM)
    pad = rows + 2 * SUB
    cells = pltpu.VMEM((EDGES, pad, LANES), F32)
    return pl.pallas_call(
        ends_kernel,
        in_specs=[vm] * 6,
        out_specs=[vm, vm],
        out_shape=[jax.ShapeDtypeStruct(mid.shape, F32), jax.ShapeDtypeStruct((LEV, 2 * SUB, LANES), F32)],
        scratch_shapes=[
            cells,
            cells,
            cells,
            cells,
            pltpu.VMEM((pad, LANES), F32),
            pltpu.VMEM((5, EDGES, pad, LANES), F32),
            pltpu.VMEM((LANES, LANES), F32),
        ],
        compiler_params=pltpu.CompilerParams(vmem_limit_bytes=VMEM_LIMIT),
        cost_estimate=pl.CostEstimate(flops=8_000_000, bytes_accessed=4_000_000, transcendentals=0),
        name="ends",
    )(ends, g0, g1, mid, norm, area)


def gather(x, idx):
    return jnp.take_along_axis(x, idx, axis=1)


def mirrored(near, far, center, ext, put):
    shape = (SUB, LANES)
    lane, at = lanes_of(shape), half_lane(shape)
    flip = SUB - 1 - lax.broadcasted_iota(jnp.int32, shape, 0)
    block = center // LANES
    first = lax.rem(center, LANES)
    own_j = first - lane
    own_i = jnp.bitwise_and(own_j, LANES - 1)
    end_j = first - jnp.where(at < EAST, at - WEST, at - EAST + LANES - OWN)
    end_i = jnp.bitwise_and(end_j, LANES - 1)

    def rows(x):
        return jnp.take_along_axis(x, flip, axis=0)

    slot = 0
    slots = []
    for k in range(ENDS):
        p, e = divmod(k, EDGES)
        slots.append((slot, slot + 1))
        for q in range(2):
            plane = p * LEV + 2 * e + q if p < 3 else 3 * LEV
            for i, rows_of in enumerate((far, far, near, near)):
                ext[i + 1, slot] = rows_of(PLANES * (i % 2) + plane)
            ext[0, slot] = roll(far(2 * PLANES + k), -(PAIR * q + WEST))
            ext[5, slot] = roll(near(2 * PLANES + k), -(PAIR * q + EAST + OWN))
            slot += 1
    for k in range(ENDS):
        p, e = divmod(k, EDGES)
        both = []
        for q in range(2):
            one, two = ext[block + 1, slots[k][q]], ext[block, slots[k][q]]
            if p < 3 or q == 0:
                plane = p * LEV + 2 * e + q if p < 3 else 3 * LEV
                put(plane, rows(jnp.where(own_j >= 0, gather(one, own_i), gather(two, own_i))))
            out = jnp.where(end_j >= 0, gather(one, end_i), gather(two, end_i))
            out = jnp.where(end_j >= LANES, gather(ext[block + 2, slots[k][q]], end_i), out)
            both.append(jnp.where(end_j < -LANES, gather(ext[block - 1, slots[k][q]], end_i), out))
        put(PLANES + k, rows(pair_up(both[0], both[1], shape)))


def band_kernel(mirror, edge, hedge, scale, old, fa, fb, *rest):
    del old
    lats, (out_ref, one, two, xb, yb, rb, coef, ext, res, sem) = rest[:-10], rest[-10:]
    side = edge.shape[1] // 2
    count = LEV + EDGES
    even = is_even("lon")
    lat_even = is_even("lat")
    is_top = lax.axis_index("lat") == lax.axis_size("lat") - 1
    lo = SUB
    north, south, own = lo + side, lo + side + SUB, lo + side + 2 * SUB
    hi = own + side
    clear_pads((one, two, xb, yb), count, lo, hi)

    def ghost(plane, of_even, of_odd):
        from_even, from_odd = [lats[i][plane] if i < len(lats) else jnp.zeros((SUB, LANES), F32) for i in (of_even, of_odd)]
        return jnp.where(lat_even, from_even, from_odd)

    def place(plane):
        if plane < 3 * LEV:
            return (one, xb, yb)[plane // LEV].at[plane % LEV]
        if plane == 3 * LEV:
            return rb.at[0]
        p, e = divmod(plane - PLANES, EDGES)
        return rb.at[1] if p == 3 else (one, xb, yb)[p].at[LEV + e]

    for plane in range(ALL):
        ref = place(plane)
        mine = edge.at[plane] if plane < PLANES else hedge.at[plane - PLANES]
        ref[pl.ds(lo, side), :] = mine[:side, :]
        ref[pl.ds(own, side), :] = mine[side:, :]
        ref[pl.ds(south, SUB), :] = ghost(plane, 1, 0)

    @pl.when(is_top)
    def _():
        def put(plane, value):
            place(plane)[pl.ds(north, SUB), :] = value

        def near(plane):
            return jnp.where(even, fa[plane], fb[plane])

        def far(plane):
            return jnp.where(even, fb[plane], fa[plane])

        mirrored(near, far, mirror[0], ext, put)

    @pl.when(jnp.logical_not(is_top))
    def _():
        for plane in range(ALL):
            place(plane)[pl.ds(north, SUB), :] = ghost(plane, 0, 1)

    n = hi - lo
    row = lo + lax.broadcasted_iota(jnp.int32, (n, LANES), 0)
    fold = is_top & (row >= north) & (row < south)
    n_far = jnp.where(is_top & (row == north - 1), 0.5, jnp.where(fold, 1.0, 0.0))
    s_far = jnp.where(is_top & (row == north), 0.5, jnp.where(fold, 1.0, 0.0))
    weights = (fold, 1.0 - n_far, n_far, 1.0 - s_far, s_far)
    for c in range(count):
        coefficients(xb, yb, rb[c // LEV, pl.ds(lo, n), :], c, lo, n, coef, weights)
    run_steps(one, two, coef, count, lo, hi, n)
    for l in range(LEV):
        for i, at in enumerate((north - SUB, own)):
            rows = pl.ds(at, SUB)
            value = merge(one[l, rows, :], one[LEV + l // 2, rows, :], l)
            res[i, l] = scale[l, i * SUB : (i + 1) * SUB, :] * value
    rows = out_ref.shape[1]
    copies = [
        pltpu.make_async_copy(res.at[0], out_ref.at[:, pl.ds(rows - SUB, SUB), :], sem.at[0]),
        pltpu.make_async_copy(res.at[1], out_ref.at[:, pl.ds(0, SUB), :], sem.at[1]),
    ]
    for copy in copies:
        copy.start()
    for copy in copies:
        copy.wait()


def band(mirror, edge, hedge, scale, out, fa, fb, lats):
    vm = pl.BlockSpec(memory_space=pltpu.VMEM)
    anywhere = pl.BlockSpec(memory_space=pl.ANY)
    pad = edge.shape[1] + 4 * SUB
    cells = pltpu.VMEM((LEV + EDGES, pad, LANES), F32)
    return pl.pallas_call(
        band_kernel,
        in_specs=[pl.BlockSpec(memory_space=pltpu.SMEM), vm, vm, vm, anywhere] + [vm] * (2 + len(lats)),
        out_specs=anywhere,
        out_shape=jax.ShapeDtypeStruct(out.shape, F32),
        input_output_aliases={4: 0},
        scratch_shapes=[
            cells,
            cells,
            cells,
            cells,
            pltpu.VMEM((2, pad, LANES), F32),
            pltpu.VMEM((5, LEV + EDGES, pad, LANES), F32),
            pltpu.VMEM((6, 2 * ENDS, SUB, LANES), F32),
            pltpu.VMEM((2, LEV, SUB, LANES), F32),
            pltpu.SemaphoreType.DMA((2,)),
        ],
        compiler_params=pltpu.CompilerParams(vmem_limit_bytes=VMEM_LIMIT),
        name="band",
    )(mirror, edge, hedge, scale, out, fa, fb, *lats)


def table(axes, sizes, send):
    place = {axis: i for i, axis in enumerate(axes)}

    def flat(lon, lat):
        spot = {"lon": lon, "lat": lat}
        index = 0
        for axis in axes:
            index = index * sizes[axis] + spot[axis]
        return index

    pairs = []
    for lon in range(sizes["lon"]):
        for lat in range(sizes["lat"]):
            to = send(lon, lat)
            if to is not None:
                pairs.append((flat(lon, lat), flat(to[0] % sizes["lon"], to[1])))
    return pairs


def per_device(axes, sizes, inc, kx, ky, mx, my, area, mask, fold_partner, norm):
    n_lon, n_lat = sizes["lon"], sizes["lat"]
    chips = n_lon // 2

    def permute(x, send):
        return lax.ppermute(x, axes, table(axes, sizes, send))

    def sibling(o, a):
        return o + 1 - 2 * (o % 2), a

    edge, m0, m1 = pack(lead(), inc, kx, ky, mx, my, area, mask)
    g0 = permute(m0, sibling)
    g1 = permute(m1, lambda o, a: (o - 1 + 2 * (o % 2), a))
    mid, ends, chip, mirror = inner(fold_partner, inc, kx, ky, mx, my, area, mask)
    edge, mid = lax.optimization_barrier((edge, mid))
    hedge, fold, *rows = edge_messages(g0, g1, edge, 1 if n_lat == 2 else 2)

    def even_lat(o, a):
        return o, a + 1 - 2 * (a % 2)

    def odd_lat(o, a):
        to = a - 1 + 2 * (a % 2)
        return (o, to) if 0 <= to < n_lat else None

    def finish(chip):
        def across(o, a):
            if a < n_lat - 1:
                return sibling(o, a)
            return (2 * ((chip - o // 2) % chips), a) if o % 2 else (2 * ((chip - 1 - o // 2) % chips) + 1, a)

        def branch(mirror, fold, rows, hedge, edge, ends, g0, g1, mid, norm, area):
            lats = [permute(x, send) for x, send in zip(rows, (even_lat, odd_lat))]
            fa = permute(fold, across)
            out, scale = lon_ends(ends, g0, g1, mid, norm, area)
            fa, scale, lats = lax.optimization_barrier((fa, scale, lats))
            fb = permute(fa, sibling)
            return band(mirror, edge, hedge, scale, out, fa, fb, lats)

        return branch

    branches = [finish(chip) for chip in range(chips)]
    return lax.switch(chip[0], branches, mirror, fold, rows, hedge, edge, ends, g0, g1, mid, norm, area)


def solution(mesh):
    axes = tuple(mesh.axis_names)
    sizes = dict(mesh.shape)
    cube, flat = P(None, "lat", "lon"), P("lat", "lon")
    return jax.shard_map(
        functools.partial(per_device, axes, sizes),
        mesh=mesh,
        in_specs=(cube, cube, cube, flat, flat, flat, cube, P("lon"), cube),
        out_specs=cube,
        check_vma=False,
    )
```

```python
import functools

import jax
import jax.numpy as jnp
from jax import lax
from jax.experimental import pallas as pl
from jax.experimental.pallas import tpu as pltpu
from jax.sharding import PartitionSpec as P

STEPS = 6
LEV = 4
LANES = 128
SUB = 8
PAIR = LANES // 2
EDGES = LEV // 2
WEST = STEPS
EAST = 4 * STEPS
OWN = 2 * STEPS
PART = 4 * STEPS * EDGES
PLANES = 3 * LEV + 1
ENDS = 3 * EDGES + 1
ALL = PLANES + ENDS
TOP = PLANES * STEPS + 2
LEAD_FLOPS = 10_000_000_000
VMEM_LIMIT = 24 * 1024 * 1024
F32 = jnp.float32


def is_even(axis):
    return lax.rem(lax.axis_index(axis), 2) == 0


def lanes_of(shape):
    return lax.broadcasted_iota(jnp.int32, shape, 1)


def roll(x, shift):
    shift = shift % LANES
    return x if shift == 0 else pltpu.roll(x, shift, 1)


def half_lane(shape):
    return jnp.bitwise_and(lanes_of(shape), PAIR - 1)


def pair_up(low, high, shape):
    return jnp.where(lanes_of(shape) < PAIR, low, high)


def own_ends(low, high):
    shape = low.shape
    at = half_lane(shape)
    west = pair_up(roll(low, WEST), roll(high, PAIR + WEST), shape)
    east = pair_up(roll(low, EAST + OWN), roll(high, PAIR + EAST + OWN), shape)
    out = jnp.where((at >= WEST) & (at < WEST + OWN), west, 0.0)
    return jnp.where((at >= EAST) & (at < EAST + OWN), east, out)


def lead_kernel(out_ref):
    out_ref[...] = jnp.zeros_like(out_ref)


def lead():
    return pl.pallas_call(
        lead_kernel,
        out_specs=pl.BlockSpec(memory_space=pltpu.VMEM),
        out_shape=jax.ShapeDtypeStruct((SUB, LANES), F32),
        compiler_params=pltpu.CompilerParams(vmem_limit_bytes=1024 * 1024),
        cost_estimate=pl.CostEstimate(flops=LEAD_FLOPS, bytes_accessed=32, transcendentals=0),
        name="lead",
    )()


def raw_fields(l, rows, inc, kx, ky, mx, my, mask, r):
    sea = mask[l, rows, :].astype(F32)
    return inc[l, rows, :] * r, kx[l, rows, :] * mx * sea, ky[l, rows, :] * my * sea


def fold_way(partner, way_ref, chip_ref, mirror_ref):
    chips = lax.axis_size("lon") // 2
    lon = lax.axis_index("lon")
    head = jnp.sum(jnp.where(lanes_of((1, LANES)) == 0, partner[...].reshape(1, LANES), 0))
    center = lax.rem(head + lon * LANES, chips * 2 * LANES)
    chip = center // (2 * LANES)
    rest = center - chip * 2 * LANES
    inside = (rest >= STEPS - 1) & (rest <= 2 * LANES - STEPS - 1)
    way_ref[...] = jnp.full((LANES,), jnp.where(inside, chip, chips), jnp.int32)
    chip_ref[...] = jnp.full((LANES,), chip, jnp.int32)
    mirror_ref[...] = jnp.full((LANES,), rest + (2 - lax.rem(lon, 2)) * LANES, jnp.int32)


def pack_kernel(start, partner, inc, kx, ky, mx, my, area, mask, edge_ref, m0_ref, m1_ref, way_ref, chip_ref, mirror_ref, acc_first, acc_last):
    del start
    fold_way(partner, way_ref, chip_ref, mirror_ref)
    rows = inc.shape[1]
    columns = m1_ref.shape[0]
    chunk = 32
    side = 2 * SUB
    even = is_even("lon")
    lane = lanes_of((chunk, LANES))
    for at in range(0, rows, chunk):
        here = pl.ds(at, chunk)
        r = 1.0 / area[here, :]
        mxv, myv = mx[here, :], my[here, :]
        first = jnp.zeros((chunk, LANES), F32)
        last = jnp.zeros((chunk, LANES), F32)
        planes = [None] * PLANES
        planes[3 * LEV] = r
        for l in range(LEV):
            fields = raw_fields(l, here, inc, kx, ky, mxv, myv, mask, r) + (r,)
            planes[l : 3 * LEV : LEV] = fields[:3]
            for p, plane in enumerate(fields):
                lane_at = PAIR * (l % 2) + 4 * STEPS * (l // 2) + STEPS * (p + 1)
                turned = roll(plane, lane_at)
                first = jnp.where((lane >= lane_at) & (lane < lane_at + STEPS), turned, first)
                last = jnp.where((lane >= lane_at - STEPS) & (lane < lane_at), turned, last)
        acc_first[here, :] = first
        acc_last[here, :] = last
        if at == 0:
            m0_ref[pl.ds(columns, 2), :] = jnp.zeros((2, LANES), F32)
            for p in range(PLANES):
                edge_ref[p, side:, :] = planes[p][:side]
        if at == rows - chunk:
            for p in range(PLANES):
                edge_ref[p, :side, :] = planes[p][chunk - side :]
                m0_ref[pl.ds(columns + 2 + STEPS * p, STEPS), :] = planes[p][chunk - STEPS :]
    for i in range(rows // LANES):
        first = jnp.transpose(acc_first[pl.ds(i * LANES, LANES), :])
        last = jnp.transpose(acc_last[pl.ds(i * LANES, LANES), :])
        for q in range(2):
            to = pl.ds((2 * i + q) * PART, PART)
            one = first[PAIR * q + STEPS : PAIR * q + STEPS + PART]
            two = last[PAIR * q : PAIR * q + PART]
            m0_ref[to, :] = jnp.where(even, two, one)
            m1_ref[to, :] = jnp.where(even, one, two)


def pack(start, partner, *fields):
    shape = fields[0].shape
    vm = pl.BlockSpec(memory_space=pltpu.VMEM)
    columns = shape[1] // LANES * 2 * PART
    acc = pltpu.VMEM(shape[1:], F32)
    return pl.pallas_call(
        pack_kernel,
        in_specs=[pl.BlockSpec(memory_space=pl.ANY)] + [vm] * 8,
        out_specs=[vm] * 6,
        out_shape=[jax.ShapeDtypeStruct((PLANES, 4 * SUB, LANES), F32)]
        + [jax.ShapeDtypeStruct((n, LANES), F32) for n in (columns + TOP, columns)]
        + [jax.ShapeDtypeStruct((LANES,), jnp.int32)] * 3,
        scratch_shapes=[acc, acc],
        compiler_params=pltpu.CompilerParams(vmem_limit_bytes=VMEM_LIMIT),
        name="pack",
    )(start, partner, *fields)


def untranspose(msg_ref, half, buf):
    buf[pl.ds(0, PART), :] = msg_ref[pl.ds(2 * PART * half, PART), :]
    buf[pl.ds(PAIR, PART), :] = msg_ref[pl.ds(2 * PART * half + PART, PART), :]
    return jnp.transpose(buf[...])


def halo_half(g0, g1, half, buf):
    t0 = untranspose(g0, half, buf)
    t1 = untranspose(g1, half, buf)
    even = is_even("lon")
    return jnp.where(even, t1, t0), jnp.where(even, t0, t1)


def with_halo(own, west_t, east_t, e, p):
    at = half_lane(own.shape)
    slot = 4 * STEPS * e + STEPS * p
    out = jnp.where(at < WEST, roll(west_t, -slot), own)
    return jnp.where((at >= EAST + OWN) & (at < EAST + OWN + STEPS), roll(east_t, EAST + OWN - slot), out)


def join_kernel(m0, g0, fold_ref):
    at = m0.shape[0] - TOP
    even = is_even("lon")
    own, other = m0[pl.ds(at, TOP), :], g0[pl.ds(at, TOP), :]
    fold_ref[pl.ds(0, TOP), :] = jnp.where(even, own, other)
    fold_ref[pl.ds(TOP, TOP), :] = jnp.where(even, other, own)


def join(m0, g0):
    vm = pl.BlockSpec(memory_space=pltpu.VMEM)
    return pl.pallas_call(
        join_kernel,
        in_specs=[vm, vm],
        out_specs=vm,
        out_shape=jax.ShapeDtypeStruct((2 * TOP, LANES), F32),
        compiler_params=pltpu.CompilerParams(vmem_limit_bytes=VMEM_LIMIT),
        name="join",
    )(m0, g0)


def join_ends_kernel(fold, hedge, out_ref):
    side = hedge.shape[1] // 2
    out_ref[pl.ds(0, 2 * TOP), :] = fold[...]
    for k in range(ENDS):
        out_ref[pl.ds(2 * TOP + SUB * k, SUB), :] = hedge[k, side - SUB : side, :]


def join_ends(fold, hedge):
    vm = pl.BlockSpec(memory_space=pltpu.VMEM)
    return pl.pallas_call(
        join_ends_kernel,
        in_specs=[vm, vm],
        out_specs=vm,
        out_shape=jax.ShapeDtypeStruct((2 * TOP + ENDS * SUB, LANES), F32),
        compiler_params=pltpu.CompilerParams(vmem_limit_bytes=VMEM_LIMIT),
        name="join_ends",
    )(fold, hedge)


def edge_kernel(g0, g1, edge, hedge_ref, *lat_refs):
    rows = edge.shape[1]
    side = rows // 2
    buf = lat_refs[-1]
    buf[...] = jnp.zeros_like(buf)
    turned = []
    for half, lo in ((1, LANES - side), (0, 0)):
        wt, et = halo_half(g0, g1, half, buf)
        turned.append((wt[lo : lo + side], et[lo : lo + side]))
    west_t, east_t = [jnp.concatenate([turned[0][i], turned[1][i]], axis=0) for i in range(2)]

    def to_lat(k, last, first):
        for ref, even_sends, odd_sends in zip(lat_refs[:-1], (last, first), (first, last)):
            ref[k] = jnp.where(is_even("lat"), even_sends, odd_sends)

    for k in range(ENDS):
        p, e = divmod(k, EDGES)
        low, high = (edge[p * LEV + 2 * e], edge[p * LEV + 2 * e + 1]) if p < 3 else (edge[3 * LEV],) * 2
        value = with_halo(own_ends(low, high), west_t, east_t, e, p)
        hedge_ref[k] = value
        to_lat(PLANES + k, value[side - SUB : side], value[side : side + SUB])
    for p in range(PLANES):
        last, first = edge[p, side - SUB : side, :], edge[p, side : side + SUB, :]
        to_lat(p, last, first)


def edge_messages(g0, g1, edge, lats):
    vm = pl.BlockSpec(memory_space=pltpu.VMEM)
    shapes = [(ENDS, edge.shape[1])] + [(ALL, SUB)] * lats
    return pl.pallas_call(
        edge_kernel,
        in_specs=[vm, vm, vm],
        out_specs=[vm] * len(shapes),
        out_shape=[jax.ShapeDtypeStruct(shape + (LANES,), F32) for shape in shapes],
        scratch_shapes=[pltpu.VMEM((LANES, LANES), F32)],
        compiler_params=pltpu.CompilerParams(vmem_limit_bytes=VMEM_LIMIT),
        name="edge",
    )(g0, g1, edge)


def coefficients(x, y, r, c, at, n, coef, weights=None):
    rows, up, down = pl.ds(at, n), pl.ds(at + 1, n), pl.ds(at - 1, n)
    here = x[c, rows, :]
    xe, xw = roll(here, -1), roll(here, 1)
    sea = jnp.where(here > 0, 1.0, 0.0)
    yv, ys = y[c, rows, :], y[c, down, :]
    east = jnp.where(xe > 0, here, 0.0)
    west = xw * sea
    north = jnp.where(x[c, up, :] > 0, yv, 0.0)
    south = ys * sea
    if weights is not None:
        flip, n_own, n_far, s_own, s_far = weights
        sea_s = jnp.where(x[c, down, :] > 0, 1.0, 0.0)
        east = jnp.where(flip, xe * sea, east)
        west = jnp.where(flip, jnp.where(xw > 0, here, 0.0), west)
        north = n_own * north + n_far * (y[c, up, :] * sea)
        south = s_own * south + s_far * (yv * sea_s)
    east, west, north, south = r * east, r * west, r * north, r * south
    coef[0, c, rows, :] = east
    coef[1, c, rows, :] = west
    coef[2, c, rows, :] = north
    coef[3, c, rows, :] = south
    coef[4, c, rows, :] = 1.0 - ((east + west) + (north + south))


def advance(src, dst, coef, c, at, n):
    rows = pl.ds(at, n)
    here = src[c, rows, :]
    lon = coef[0, c, rows, :] * roll(here, -1) + coef[1, c, rows, :] * roll(here, 1)
    lat = coef[2, c, rows, :] * src[c, pl.ds(at + 1, n), :] + coef[3, c, rows, :] * src[c, pl.ds(at - 1, n), :]
    dst[c, rows, :] = coef[4, c, rows, :] * here + (lon + lat)


def run_steps(one, two, coef, count, lo, hi, n):
    def both(_, carry):
        for src, dst in ((one, two), (two, one)):
            for at in range(lo, hi, n):
                for c in range(count):
                    advance(src, dst, coef, c, at, n)
        return carry

    lax.fori_loop(0, STEPS // 2, both, 0)


def clear_pads(refs, count, lo, hi):
    zero = jnp.zeros((SUB, LANES), F32)
    for ref in refs:
        for c in range(count):
            ref[c, pl.ds(lo - SUB, SUB), :] = zero
            ref[c, pl.ds(hi, SUB), :] = zero


def inner_kernel(inc, kx, ky, mx, my, area, mask, out_ref, ends_ref, one, two, xb, yb, rb, coef):
    rows = inc.shape[1]
    n = 16
    lo, hi = SUB, SUB + rows
    clear_pads((one, two, xb, yb), LEV, lo, hi)
    for at in range(0, rows, n):
        here, there = pl.ds(at, n), pl.ds(lo + at, n)
        r = 1.0 / area[here, :]
        rb[here, :] = r
        mxv, myv = mx[here, :], my[here, :]
        fields = [raw_fields(l, here, inc, kx, ky, mxv, myv, mask, r) for l in range(LEV)]
        for l in range(LEV):
            one[l, there, :], xb[l, there, :], yb[l, there, :] = fields[l]
        for e in range(EDGES):
            for p in range(3):
                ends_ref[p * EDGES + e, here, :] = own_ends(fields[2 * e][p], fields[2 * e + 1][p])
        ends_ref[3 * EDGES, here, :] = own_ends(r, r)
    for at in range(lo, hi, n):
        for l in range(LEV):
            coefficients(xb, yb, rb[pl.ds(at - lo, n), :], l, at, n, coef)
    run_steps(one, two, coef, LEV, lo, hi, n)
    for l in range(LEV):
        out_ref[l] = one[l, pl.ds(lo, rows), :]


def inner(*fields):
    shape = fields[0].shape
    rows = shape[1]
    vm = pl.BlockSpec(memory_space=pltpu.VMEM)
    pad = rows + 2 * SUB
    cells = pltpu.VMEM((LEV, pad, LANES), F32)
    return pl.pallas_call(
        inner_kernel,
        in_specs=[vm] * 7,
        out_specs=[vm, vm],
        out_shape=[
            jax.ShapeDtypeStruct(shape, F32),
            jax.ShapeDtypeStruct((ENDS, rows, LANES), F32),
        ],
        scratch_shapes=[
            cells,
            cells,
            cells,
            cells,
            pltpu.VMEM((rows, LANES), F32),
            pltpu.VMEM((5, LEV, pad, LANES), F32),
        ],
        compiler_params=pltpu.CompilerParams(vmem_limit_bytes=VMEM_LIMIT),
        cost_estimate=pl.CostEstimate(flops=12_000_000, bytes_accessed=6_000_000, transcendentals=0),
        name="inner",
    )(*fields)


def merge(own, ends, l):
    lane = lanes_of(own.shape)
    at = PAIR * (l % 2)
    out = jnp.where(lane < STEPS, roll(ends, -(at + WEST)), own)
    return jnp.where(lane >= LANES - STEPS, roll(ends, -(at + EAST + OWN)), out)


def ends_kernel(ends, g0, g1, mid, norm, area, out_ref, scale_ref, one, two, xb, yb, rb, coef, buf):
    rows = mid.shape[1]
    n = 16
    lo, hi = SUB, SUB + rows
    buf[...] = jnp.zeros_like(buf)
    clear_pads((one, two, xb, yb), EDGES, lo, hi)
    for half in range(2):
        wt, et = halo_half(g0, g1, half, buf)
        here, there = pl.ds(half * LANES, LANES), pl.ds(lo + half * LANES, LANES)
        for e in range(EDGES):
            one[e, there, :] = with_halo(ends[e, here, :], wt, et, e, 0)
            xb[e, there, :] = with_halo(ends[EDGES + e, here, :], wt, et, e, 1)
            yb[e, there, :] = with_halo(ends[2 * EDGES + e, here, :], wt, et, e, 2)
        rb[there, :] = with_halo(ends[3 * EDGES, here, :], wt, et, 0, 3)
    for at in range(lo, hi, n):
        for e in range(EDGES):
            coefficients(xb, yb, rb[pl.ds(at, n), :], e, at, n, coef)
    run_steps(one, two, coef, EDGES, lo, hi, n)
    for l in range(LEV):
        scale = norm[l] * area[...]
        out_ref[l] = scale * merge(mid[l], one[l // 2, pl.ds(lo, rows), :], l)
        scale_ref[l, :SUB, :] = scale[rows - SUB :]
        scale_ref[l, SUB:, :] = scale[:SUB]


def lon_ends(ends, g0, g1, mid, norm, area):
    rows = mid.shape[1]
    vm = pl.BlockSpec(memory_space=pltpu.VMEM)
    pad = rows + 2 * SUB
    cells = pltpu.VMEM((EDGES, pad, LANES), F32)
    return pl.pallas_call(
        ends_kernel,
        in_specs=[vm] * 6,
        out_specs=[vm, vm],
        out_shape=[jax.ShapeDtypeStruct(mid.shape, F32), jax.ShapeDtypeStruct((LEV, 2 * SUB, LANES), F32)],
        scratch_shapes=[
            cells,
            cells,
            cells,
            cells,
            pltpu.VMEM((pad, LANES), F32),
            pltpu.VMEM((5, EDGES, pad, LANES), F32),
            pltpu.VMEM((LANES, LANES), F32),
        ],
        compiler_params=pltpu.CompilerParams(vmem_limit_bytes=VMEM_LIMIT),
        cost_estimate=pl.CostEstimate(flops=8_000_000, bytes_accessed=4_000_000, transcendentals=0),
        name="ends",
    )(ends, g0, g1, mid, norm, area)


def gather(x, idx):
    return jnp.take_along_axis(x, idx, axis=1)


def mirrored(near, far, far_ends, center, ext, put):
    shape = (SUB, LANES)
    lane, at = lanes_of(shape), half_lane(shape)
    flip = SUB - 1 - lax.broadcasted_iota(jnp.int32, shape, 0)
    block = center // LANES
    first = lax.rem(center, LANES)
    own_j = first - lane
    own_i = jnp.bitwise_and(own_j, LANES - 1)
    end_j = first - jnp.where(at < EAST, at - WEST, at - EAST + LANES - OWN)
    end_i = jnp.bitwise_and(end_j, LANES - 1)

    def rows(x):
        return jnp.take_along_axis(x, flip, axis=0)

    for at, rows_of in ((1, far), (3, near)):
        for slot in range(2 * ENDS):
            p, l = divmod(slot, LEV)
            for q in range(2):
                ext[at + q, slot] = rows_of(TOP * q + STEPS * (3 * LEV if p == 3 else slot))
    if far_ends:
        for slot in range(2 * ENDS):
            k, q = divmod(slot, 2)
            ext[0, slot] = roll(far(2 * TOP + SUB * k), -(PAIR * q + WEST))
            ext[5, slot] = roll(near(2 * TOP + SUB * k), -(PAIR * q + EAST + OWN))
    for k in range(ENDS):
        p, e = divmod(k, EDGES)
        both = []
        for q in range(2):
            slot = 2 * k + q
            one, two = ext[block + 1, slot], ext[block, slot]
            if p < 3 or q == 0:
                plane = p * LEV + 2 * e + q if p < 3 else 3 * LEV
                put(plane, rows(jnp.where(own_j >= 0, gather(one, own_i), gather(two, own_i))))
            out = jnp.where(end_j >= 0, gather(one, end_i), gather(two, end_i))
            out = jnp.where(end_j >= LANES, gather(ext[block + 2, slot], end_i), out)
            both.append(jnp.where(end_j < -LANES, gather(ext[block - 1, slot], end_i), out))
        put(PLANES + k, rows(pair_up(both[0], both[1], shape)))


def band_kernel(mirror, edge, hedge, scale, body, fa, fb, *rest):
    lats, (out_ref, one, two, xb, yb, rb, coef, ext, res, sem) = rest[:-10], rest[-10:]
    inner_rows = pl.ds(SUB, body.shape[1] - 2 * SUB)
    copies = [pltpu.make_async_copy(body.at[:, inner_rows, :], out_ref.at[:, inner_rows, :], sem.at[2])]
    copies[0].start()
    side = edge.shape[1] // 2
    count = LEV + EDGES
    even = is_even("lon")
    lat_even = is_even("lat")
    is_top = lax.axis_index("lat") == lax.axis_size("lat") - 1
    lo = SUB
    north, south, own = lo + side, lo + side + SUB, lo + side + 2 * SUB
    hi = own + side
    clear_pads((one, two, xb, yb), count, lo, hi)

    def ghost(plane, of_even, of_odd):
        from_even, from_odd = [lats[i][plane] if i < len(lats) else jnp.zeros((SUB, LANES), F32) for i in (of_even, of_odd)]
        return jnp.where(lat_even, from_even, from_odd)

    def place(plane):
        if plane < 3 * LEV:
            return (one, xb, yb)[plane // LEV].at[plane % LEV]
        if plane == 3 * LEV:
            return rb.at[0]
        p, e = divmod(plane - PLANES, EDGES)
        return rb.at[1] if p == 3 else (one, xb, yb)[p].at[LEV + e]

    for plane in range(ALL):
        ref = place(plane)
        mine = edge.at[plane] if plane < PLANES else hedge.at[plane - PLANES]
        ref[pl.ds(lo, side), :] = mine[:side, :]
        ref[pl.ds(own, side), :] = mine[side:, :]
        ref[pl.ds(south, SUB), :] = ghost(plane, 1, 0)

    @pl.when(is_top)
    def _():
        def put(plane, value):
            place(plane)[pl.ds(north, SUB), :] = value

        def near(at):
            return jnp.where(even, fa[pl.ds(at, SUB), :], fb[pl.ds(at, SUB), :])

        def far(at):
            return jnp.where(even, fb[pl.ds(at, SUB), :], fa[pl.ds(at, SUB), :])

        center = jnp.max(mirror[...].reshape(1, LANES))
        mirrored(near, far, fa.shape[0] > 2 * TOP, center, ext, put)

    @pl.when(jnp.logical_not(is_top))
    def _():
        for plane in range(ALL):
            place(plane)[pl.ds(north, SUB), :] = ghost(plane, 0, 1)

    n = hi - lo
    row = lo + lax.broadcasted_iota(jnp.int32, (n, LANES), 0)
    fold = is_top & (row >= north) & (row < south)
    n_far = jnp.where(is_top & (row == north - 1), 0.5, jnp.where(fold, 1.0, 0.0))
    s_far = jnp.where(is_top & (row == north), 0.5, jnp.where(fold, 1.0, 0.0))
    weights = (fold, 1.0 - n_far, n_far, 1.0 - s_far, s_far)
    for c in range(count):
        coefficients(xb, yb, rb[c // LEV, pl.ds(lo, n), :], c, lo, n, coef, weights)
    run_steps(one, two, coef, count, lo, hi, n)
    for l in range(LEV):
        for i, at in enumerate((north - SUB, own)):
            rows = pl.ds(at, SUB)
            value = merge(one[l, rows, :], one[LEV + l // 2, rows, :], l)
            res[i, l] = scale[l, i * SUB : (i + 1) * SUB, :] * value
    rows = out_ref.shape[1]
    copies += [
        pltpu.make_async_copy(res.at[0], out_ref.at[:, pl.ds(rows - SUB, SUB), :], sem.at[0]),
        pltpu.make_async_copy(res.at[1], out_ref.at[:, pl.ds(0, SUB), :], sem.at[1]),
    ]
    for copy in copies[1:]:
        copy.start()
    for copy in copies:
        copy.wait()


def band(mirror, edge, hedge, scale, body, fa, fb, lats):
    vm = pl.BlockSpec(memory_space=pltpu.VMEM)
    anywhere = pl.BlockSpec(memory_space=pl.ANY)
    pad = edge.shape[1] + 4 * SUB
    cells = pltpu.VMEM((LEV + EDGES, pad, LANES), F32)
    return pl.pallas_call(
        band_kernel,
        in_specs=[vm] * (7 + len(lats)),
        out_specs=anywhere,
        out_shape=pltpu.HBM(body.shape, F32),
        scratch_shapes=[
            cells,
            cells,
            cells,
            cells,
            pltpu.VMEM((2, pad, LANES), F32),
            pltpu.VMEM((5, LEV + EDGES, pad, LANES), F32),
            pltpu.VMEM((6, 2 * ENDS, SUB, LANES), F32),
            pltpu.VMEM((2, LEV, SUB, LANES), F32),
            pltpu.SemaphoreType.DMA((3,)),
        ],
        compiler_params=pltpu.CompilerParams(vmem_limit_bytes=VMEM_LIMIT),
        name="band",
    )(mirror, edge, hedge, scale, body, fa, fb, *lats)


def table(axes, sizes, send):
    place = {axis: i for i, axis in enumerate(axes)}

    def flat(lon, lat):
        spot = {"lon": lon, "lat": lat}
        index = 0
        for axis in axes:
            index = index * sizes[axis] + spot[axis]
        return index

    pairs = []
    for lon in range(sizes["lon"]):
        for lat in range(sizes["lat"]):
            to = send(lon, lat)
            if to is not None:
                pairs.append((flat(lon, lat), flat(to[0] % sizes["lon"], to[1])))
    return pairs


def per_device(axes, sizes, inc, kx, ky, mx, my, area, mask, fold_partner, norm):
    n_lon, n_lat = sizes["lon"], sizes["lat"]
    chips = n_lon // 2

    def permute(x, send):
        return lax.ppermute(x, axes, table(axes, sizes, send))

    def sibling(o, a):
        return o + 1 - 2 * (o % 2), a

    def outer(o, a):
        return o - 1 + 2 * (o % 2), a

    def even_lat(o, a):
        return o, a + 1 - 2 * (a % 2)

    def odd_lat(o, a):
        to = a - 1 + 2 * (a % 2)
        return (o, to) if 0 <= to < n_lat else None

    def across(chip):
        def send(o, a):
            if a < n_lat - 1:
                return sibling(o, a)
            return (2 * ((chip - o // 2) % chips), a) if o % 2 else (2 * ((chip - 1 - o // 2) % chips) + 1, a)

        return lambda x: permute(x, send)

    def finish(over_fold):
        def branch(m0, m1, edge, chip, mirror, fields, norm):
            g0 = permute(m0, sibling)
            g1 = permute(m1, outer)
            fold = join(m0, g0)
            if over_fold is not None:
                fa = over_fold(fold)
                fold, fields = lax.optimization_barrier((fold, fields))
            mid, ends = inner(*fields)
            edge, mid = lax.optimization_barrier((edge, mid))
            hedge, *rows = edge_messages(g0, g1, edge, 1 if n_lat == 2 else 2)
            if over_fold is None:
                fa = lax.switch(chip[0], [across(i) for i in range(chips)], join_ends(fold, hedge))
            lats = [permute(x, send) for x, send in zip(rows, (even_lat, odd_lat))]
            body, scale = lon_ends(ends, g0, g1, mid, norm, fields[5])
            fa, scale, lats = lax.optimization_barrier((fa, scale, lats))
            fb = permute(fa, sibling)
            return band(mirror, edge, hedge, scale, body, fa, fb, lats)

        return branch

    fields = (inc, kx, ky, mx, my, area, mask)
    edge, m0, m1, way, chip, mirror = pack(lead(), fold_partner, *fields)
    branches = [finish(across(i)) for i in range(chips)] + [finish(None)]
    return lax.switch(way[0], branches, m0, m1, edge, chip, mirror, fields, norm)


def solution(mesh):
    axes = tuple(mesh.axis_names)
    sizes = dict(mesh.shape)
    cube, flat = P(None, "lat", "lon"), P("lat", "lon")
    return jax.shard_map(
        functools.partial(per_device, axes, sizes),
        mesh=mesh,
        in_specs=(cube, cube, cube, flat, flat, flat, cube, P("lon"), cube),
        out_specs=cube,
        check_vma=False,
    )
```

```python
import functools

import jax
import jax.numpy as jnp
from jax import lax
from jax.experimental import pallas as pl
from jax.experimental.pallas import tpu as pltpu
from jax.sharding import PartitionSpec as P

STEPS = 6
LEV = 4
LANES = 128
SUB = 8
PAIR = LANES // 2
EDGES = LEV // 2
WEST = STEPS
EAST = 4 * STEPS
OWN = 2 * STEPS
PART = 4 * STEPS * EDGES
PLANES = 3 * LEV + 1
ENDS = 3 * EDGES + 1
ALL = PLANES + ENDS
TOP = PLANES * STEPS + 2
PREP = 4
LEAD_FLOPS = 10_000_000_000
VMEM_LIMIT = 24 * 1024 * 1024
F32 = jnp.float32


def is_even(axis):
    return lax.rem(lax.axis_index(axis), 2) == 0


def lanes_of(shape):
    return lax.broadcasted_iota(jnp.int32, shape, 1)


def roll(x, shift):
    shift = shift % LANES
    return x if shift == 0 else pltpu.roll(x, shift, 1)


def half_lane(shape):
    return jnp.bitwise_and(lanes_of(shape), PAIR - 1)


def pair_up(low, high, shape):
    return jnp.where(lanes_of(shape) < PAIR, low, high)


def own_ends(low, high):
    shape = low.shape
    at = half_lane(shape)
    west = pair_up(roll(low, WEST), roll(high, PAIR + WEST), shape)
    east = pair_up(roll(low, EAST + OWN), roll(high, PAIR + EAST + OWN), shape)
    out = jnp.where((at >= WEST) & (at < WEST + OWN), west, 0.0)
    return jnp.where((at >= EAST) & (at < EAST + OWN), east, out)


def lead_kernel(out_ref):
    out_ref[...] = jnp.zeros_like(out_ref)


def lead():
    return pl.pallas_call(
        lead_kernel,
        out_specs=pl.BlockSpec(memory_space=pltpu.VMEM),
        out_shape=jax.ShapeDtypeStruct((SUB, LANES), F32),
        compiler_params=pltpu.CompilerParams(vmem_limit_bytes=1024 * 1024),
        cost_estimate=pl.CostEstimate(flops=LEAD_FLOPS, bytes_accessed=32, transcendentals=0),
        name="lead",
    )()


def raw_fields(l, rows, inc, kx, ky, mx, my, mask, r):
    sea = mask[l, rows, :].astype(F32)
    return inc[l, rows, :] * r, kx[l, rows, :] * mx * sea, ky[l, rows, :] * my * sea


def fold_way(partner, way_ref, chip_ref, mirror_ref):
    chips = lax.axis_size("lon") // 2
    lon = lax.axis_index("lon")
    head = jnp.sum(jnp.where(lanes_of((1, LANES)) == 0, partner[...].reshape(1, LANES), 0))
    center = lax.rem(head + lon * LANES, chips * 2 * LANES)
    chip = center // (2 * LANES)
    rest = center - chip * 2 * LANES
    inside = (rest >= STEPS - 1) & (rest <= 2 * LANES - STEPS - 1)
    way_ref[...] = jnp.full((LANES,), jnp.where(inside, chip, chips), jnp.int32)
    chip_ref[...] = jnp.full((LANES,), chip, jnp.int32)
    mirror_ref[...] = jnp.full((LANES,), rest + (2 - lax.rem(lon, 2)) * LANES, jnp.int32)


def pack_kernel(start, partner, inc, kx, ky, mx, my, area, mask, edge_ref, m0_ref, m1_ref, way_ref, chip_ref, mirror_ref, acc_first, acc_last):
    del start
    fold_way(partner, way_ref, chip_ref, mirror_ref)
    rows = inc.shape[1]
    columns = m1_ref.shape[0]
    chunk = 32
    side = 2 * SUB
    even = is_even("lon")
    lane = lanes_of((chunk, LANES))
    for at in range(0, rows, chunk):
        here = pl.ds(at, chunk)
        r = 1.0 / area[here, :]
        mxv, myv = mx[here, :], my[here, :]
        first = jnp.zeros((chunk, LANES), F32)
        last = jnp.zeros((chunk, LANES), F32)
        planes = [None] * PLANES
        planes[3 * LEV] = r
        for l in range(LEV):
            fields = raw_fields(l, here, inc, kx, ky, mxv, myv, mask, r) + (r,)
            planes[l : 3 * LEV : LEV] = fields[:3]
            for p, plane in enumerate(fields):
                lane_at = PAIR * (l % 2) + 4 * STEPS * (l // 2) + STEPS * (p + 1)
                turned = roll(plane, lane_at)
                first = jnp.where((lane >= lane_at) & (lane < lane_at + STEPS), turned, first)
                last = jnp.where((lane >= lane_at - STEPS) & (lane < lane_at), turned, last)
        acc_first[here, :] = first
        acc_last[here, :] = last
        if at == 0:
            m0_ref[pl.ds(columns, 2), :] = jnp.zeros((2, LANES), F32)
            for p in range(PLANES):
                edge_ref[p, side:, :] = planes[p][:side]
        if at == rows - chunk:
            for p in range(PLANES):
                edge_ref[p, :side, :] = planes[p][chunk - side :]
                m0_ref[pl.ds(columns + 2 + STEPS * p, STEPS), :] = planes[p][chunk - STEPS :]
    for i in range(rows // LANES):
        first = jnp.transpose(acc_first[pl.ds(i * LANES, LANES), :])
        last = jnp.transpose(acc_last[pl.ds(i * LANES, LANES), :])
        for q in range(2):
            to = pl.ds((2 * i + q) * PART, PART)
            one = first[PAIR * q + STEPS : PAIR * q + STEPS + PART]
            two = last[PAIR * q : PAIR * q + PART]
            m0_ref[to, :] = jnp.where(even, two, one)
            m1_ref[to, :] = jnp.where(even, one, two)


def pack(start, partner, *fields):
    shape = fields[0].shape
    vm = pl.BlockSpec(memory_space=pltpu.VMEM)
    columns = shape[1] // LANES * 2 * PART
    acc = pltpu.VMEM(shape[1:], F32)
    return pl.pallas_call(
        pack_kernel,
        in_specs=[pl.BlockSpec(memory_space=pl.ANY)] + [vm] * 8,
        out_specs=[vm] * 6,
        out_shape=[jax.ShapeDtypeStruct((PLANES, 4 * SUB, LANES), F32)]
        + [jax.ShapeDtypeStruct((n, LANES), F32) for n in (columns + TOP, columns)]
        + [jax.ShapeDtypeStruct((LANES,), jnp.int32)] * 3,
        scratch_shapes=[acc, acc],
        compiler_params=pltpu.CompilerParams(vmem_limit_bytes=VMEM_LIMIT),
        name="pack",
    )(start, partner, *fields)


def untranspose(msg_ref, half, buf):
    buf[pl.ds(0, PART), :] = msg_ref[pl.ds(2 * PART * half, PART), :]
    buf[pl.ds(PAIR, PART), :] = msg_ref[pl.ds(2 * PART * half + PART, PART), :]
    return jnp.transpose(buf[...])


def halo_half(g0, g1, half, buf):
    t0 = untranspose(g0, half, buf)
    t1 = untranspose(g1, half, buf)
    even = is_even("lon")
    return jnp.where(even, t1, t0), jnp.where(even, t0, t1)


def with_halo(own, west_t, east_t, e, p):
    at = half_lane(own.shape)
    slot = 4 * STEPS * e + STEPS * p
    out = jnp.where(at < WEST, roll(west_t, -slot), own)
    return jnp.where((at >= EAST + OWN) & (at < EAST + OWN + STEPS), roll(east_t, EAST + OWN - slot), out)


def join_kernel(m0, g0, fold_ref):
    at = m0.shape[0] - TOP
    even = is_even("lon")
    own, other = m0[pl.ds(at, TOP), :], g0[pl.ds(at, TOP), :]
    fold_ref[pl.ds(0, TOP), :] = jnp.where(even, own, other)
    fold_ref[pl.ds(TOP, TOP), :] = jnp.where(even, other, own)


def join(m0, g0):
    vm = pl.BlockSpec(memory_space=pltpu.VMEM)
    return pl.pallas_call(
        join_kernel,
        in_specs=[vm, vm],
        out_specs=vm,
        out_shape=jax.ShapeDtypeStruct((2 * TOP, LANES), F32),
        compiler_params=pltpu.CompilerParams(vmem_limit_bytes=VMEM_LIMIT),
        name="join",
    )(m0, g0)


def join_ends_kernel(fold, hedge, out_ref):
    side = hedge.shape[1] // 2
    out_ref[pl.ds(0, 2 * TOP), :] = fold[...]
    for k in range(ENDS):
        out_ref[pl.ds(2 * TOP + SUB * k, SUB), :] = hedge[k, side - SUB : side, :]


def join_ends(fold, hedge):
    vm = pl.BlockSpec(memory_space=pltpu.VMEM)
    return pl.pallas_call(
        join_ends_kernel,
        in_specs=[vm, vm],
        out_specs=vm,
        out_shape=jax.ShapeDtypeStruct((2 * TOP + ENDS * SUB, LANES), F32),
        compiler_params=pltpu.CompilerParams(vmem_limit_bytes=VMEM_LIMIT),
        name="join_ends",
    )(fold, hedge)


def edge_kernel(g0, g1, edge, hedge_ref, *lat_refs):
    rows = edge.shape[1]
    side = rows // 2
    buf = lat_refs[-1]
    buf[...] = jnp.zeros_like(buf)
    turned = []
    for half, lo in ((1, LANES - side), (0, 0)):
        wt, et = halo_half(g0, g1, half, buf)
        turned.append((wt[lo : lo + side], et[lo : lo + side]))
    west_t, east_t = [jnp.concatenate([turned[0][i], turned[1][i]], axis=0) for i in range(2)]

    def to_lat(k, last, first):
        for ref, even_sends, odd_sends in zip(lat_refs[:-1], (last, first), (first, last)):
            ref[k] = jnp.where(is_even("lat"), even_sends, odd_sends)

    for k in range(ENDS):
        p, e = divmod(k, EDGES)
        low, high = (edge[p * LEV + 2 * e], edge[p * LEV + 2 * e + 1]) if p < 3 else (edge[3 * LEV],) * 2
        value = with_halo(own_ends(low, high), west_t, east_t, e, p)
        hedge_ref[k] = value
        to_lat(PLANES + k, value[side - SUB : side], value[side : side + SUB])
    for p in range(PLANES):
        last, first = edge[p, side - SUB : side, :], edge[p, side : side + SUB, :]
        to_lat(p, last, first)


def edge_messages(g0, g1, edge, lats):
    vm = pl.BlockSpec(memory_space=pltpu.VMEM)
    shapes = [(ENDS, edge.shape[1])] + [(ALL, SUB)] * lats
    return pl.pallas_call(
        edge_kernel,
        in_specs=[vm, vm, vm],
        out_specs=[vm] * len(shapes),
        out_shape=[jax.ShapeDtypeStruct(shape + (LANES,), F32) for shape in shapes],
        scratch_shapes=[pltpu.VMEM((LANES, LANES), F32)],
        compiler_params=pltpu.CompilerParams(vmem_limit_bytes=VMEM_LIMIT),
        name="edge",
    )(g0, g1, edge)


def coefficients(x, y, r, c, at, n, coef, weights=None):
    rows, up, down = pl.ds(at, n), pl.ds(at + 1, n), pl.ds(at - 1, n)
    here = x[c, rows, :]
    xe, xw = roll(here, -1), roll(here, 1)
    sea = jnp.where(here > 0, 1.0, 0.0)
    yv, ys = y[c, rows, :], y[c, down, :]
    east = jnp.where(xe > 0, here, 0.0)
    west = xw * sea
    north = jnp.where(x[c, up, :] > 0, yv, 0.0)
    south = ys * sea
    if weights is not None:
        flip, n_own, n_far, s_own, s_far = weights
        sea_s = jnp.where(x[c, down, :] > 0, 1.0, 0.0)
        east = jnp.where(flip, xe * sea, east)
        west = jnp.where(flip, jnp.where(xw > 0, here, 0.0), west)
        north = n_own * north + n_far * (y[c, up, :] * sea)
        south = s_own * south + s_far * (yv * sea_s)
    east, west, north, south = r * east, r * west, r * north, r * south
    coef[0, c, rows, :] = east
    coef[1, c, rows, :] = west
    coef[2, c, rows, :] = north
    coef[3, c, rows, :] = south
    coef[4, c, rows, :] = 1.0 - ((east + west) + (north + south))


def advance(src, dst, coef, c, at, n):
    rows = pl.ds(at, n)
    here = src[c, rows, :]
    lon = coef[0, c, rows, :] * roll(here, -1) + coef[1, c, rows, :] * roll(here, 1)
    lat = coef[2, c, rows, :] * src[c, pl.ds(at + 1, n), :] + coef[3, c, rows, :] * src[c, pl.ds(at - 1, n), :]
    dst[c, rows, :] = coef[4, c, rows, :] * here + (lon + lat)


def run_steps(one, two, coef, count, lo, hi, n):
    def both(_, carry):
        for src, dst in ((one, two), (two, one)):
            for at in range(lo, hi, n):
                for c in range(count):
                    advance(src, dst, coef, c, at, n)
        return carry

    lax.fori_loop(0, STEPS // 2, both, 0)


def clear_pads(refs, count, lo, hi):
    zero = jnp.zeros((SUB, LANES), F32)
    for ref in refs:
        for c in range(count):
            ref[c, pl.ds(lo - SUB, SUB), :] = zero
            ref[c, pl.ds(hi, SUB), :] = zero


def inner_kernel(inc, kx, ky, mx, my, area, mask, out_ref, ends_ref, one, two, xb, yb, rb, coef):
    rows = inc.shape[1]
    n = 16
    lo, hi = SUB, SUB + rows
    clear_pads((one, two, xb, yb), LEV, lo, hi)
    span = rows // PREP

    def prepare(i, carry):
        for at in range(0, span, n):
            at = pl.multiple_of(i * span + at, n)
            prepare_rows(pl.ds(at, n), pl.ds(lo + at, n))
        return carry

    def prepare_rows(here, there):
        r = 1.0 / area[here, :]
        rb[here, :] = r
        mxv, myv = mx[here, :], my[here, :]
        fields = [raw_fields(l, here, inc, kx, ky, mxv, myv, mask, r) for l in range(LEV)]
        for l in range(LEV):
            one[l, there, :], xb[l, there, :], yb[l, there, :] = fields[l]
        for e in range(EDGES):
            for p in range(3):
                ends_ref[p * EDGES + e, here, :] = own_ends(fields[2 * e][p], fields[2 * e + 1][p])
        ends_ref[3 * EDGES, here, :] = own_ends(r, r)
    def combine(i, carry):
        for at in range(0, span, n):
            at = pl.multiple_of(i * span + at, n)
            for l in range(LEV):
                coefficients(xb, yb, rb[pl.ds(at, n), :], l, lo + at, n, coef)
        return carry

    lax.fori_loop(0, PREP, prepare, 0)
    lax.fori_loop(0, PREP, combine, 0)
    run_steps(one, two, coef, LEV, lo, hi, n)
    for l in range(LEV):
        out_ref[l] = one[l, pl.ds(lo, rows), :]


def inner(*fields):
    shape = fields[0].shape
    rows = shape[1]
    vm = pl.BlockSpec(memory_space=pltpu.VMEM)
    pad = rows + 2 * SUB
    cells = pltpu.VMEM((LEV, pad, LANES), F32)
    return pl.pallas_call(
        inner_kernel,
        in_specs=[vm] * 7,
        out_specs=[vm, vm],
        out_shape=[
            jax.ShapeDtypeStruct(shape, F32),
            jax.ShapeDtypeStruct((ENDS, rows, LANES), F32),
        ],
        scratch_shapes=[
            cells,
            cells,
            cells,
            cells,
            pltpu.VMEM((rows, LANES), F32),
            pltpu.VMEM((5, LEV, pad, LANES), F32),
        ],
        compiler_params=pltpu.CompilerParams(vmem_limit_bytes=VMEM_LIMIT),
        cost_estimate=pl.CostEstimate(flops=12_000_000, bytes_accessed=6_000_000, transcendentals=0),
        name="inner",
    )(*fields)


def merge(own, ends, l):
    lane = lanes_of(own.shape)
    at = PAIR * (l % 2)
    out = jnp.where(lane < STEPS, roll(ends, -(at + WEST)), own)
    return jnp.where(lane >= LANES - STEPS, roll(ends, -(at + EAST + OWN)), out)


def ends_kernel(ends, g0, g1, mid, norm, area, out_ref, scale_ref, one, two, xb, yb, rb, coef, buf):
    rows = mid.shape[1]
    n = 16
    lo, hi = SUB, SUB + rows
    buf[...] = jnp.zeros_like(buf)
    clear_pads((one, two, xb, yb), EDGES, lo, hi)
    for half in range(2):
        wt, et = halo_half(g0, g1, half, buf)
        here, there = pl.ds(half * LANES, LANES), pl.ds(lo + half * LANES, LANES)
        for e in range(EDGES):
            one[e, there, :] = with_halo(ends[e, here, :], wt, et, e, 0)
            xb[e, there, :] = with_halo(ends[EDGES + e, here, :], wt, et, e, 1)
            yb[e, there, :] = with_halo(ends[2 * EDGES + e, here, :], wt, et, e, 2)
        rb[there, :] = with_halo(ends[3 * EDGES, here, :], wt, et, 0, 3)
    for at in range(lo, hi, n):
        for e in range(EDGES):
            coefficients(xb, yb, rb[pl.ds(at, n), :], e, at, n, coef)
    run_steps(one, two, coef, EDGES, lo, hi, n)
    for l in range(LEV):
        scale = norm[l] * area[...]
        out_ref[l] = scale * merge(mid[l], one[l // 2, pl.ds(lo, rows), :], l)
        scale_ref[l, :SUB, :] = scale[rows - SUB :]
        scale_ref[l, SUB:, :] = scale[:SUB]


def lon_ends(ends, g0, g1, mid, norm, area):
    rows = mid.shape[1]
    vm = pl.BlockSpec(memory_space=pltpu.VMEM)
    pad = rows + 2 * SUB
    cells = pltpu.VMEM((EDGES, pad, LANES), F32)
    return pl.pallas_call(
        ends_kernel,
        in_specs=[vm] * 6,
        out_specs=[vm, vm],
        out_shape=[jax.ShapeDtypeStruct(mid.shape, F32), jax.ShapeDtypeStruct((LEV, 2 * SUB, LANES), F32)],
        scratch_shapes=[
            cells,
            cells,
            cells,
            cells,
            pltpu.VMEM((pad, LANES), F32),
            pltpu.VMEM((5, EDGES, pad, LANES), F32),
            pltpu.VMEM((LANES, LANES), F32),
        ],
        compiler_params=pltpu.CompilerParams(vmem_limit_bytes=VMEM_LIMIT),
        cost_estimate=pl.CostEstimate(flops=8_000_000, bytes_accessed=4_000_000, transcendentals=0),
        name="ends",
    )(ends, g0, g1, mid, norm, area)


def gather(x, idx):
    return jnp.take_along_axis(x, idx, axis=1)


def mirrored(near, far, far_ends, center, ext, put):
    shape = (SUB, LANES)
    lane, at = lanes_of(shape), half_lane(shape)
    flip = SUB - 1 - lax.broadcasted_iota(jnp.int32, shape, 0)
    block = center // LANES
    first = lax.rem(center, LANES)
    own_j = first - lane
    own_i = jnp.bitwise_and(own_j, LANES - 1)
    end_j = first - jnp.where(at < EAST, at - WEST, at - EAST + LANES - OWN)
    end_i = jnp.bitwise_and(end_j, LANES - 1)

    def rows(x):
        return jnp.take_along_axis(x, flip, axis=0)

    for at, rows_of in ((1, far), (3, near)):
        for slot in range(2 * ENDS):
            p, l = divmod(slot, LEV)
            for q in range(2):
                ext[at + q, slot] = rows_of(TOP * q + STEPS * (3 * LEV if p == 3 else slot))
    if far_ends:
        for slot in range(2 * ENDS):
            k, q = divmod(slot, 2)
            ext[0, slot] = roll(far(2 * TOP + SUB * k), -(PAIR * q + WEST))
            ext[5, slot] = roll(near(2 * TOP + SUB * k), -(PAIR * q + EAST + OWN))
    for k in range(ENDS):
        p, e = divmod(k, EDGES)
        both = []
        for q in range(2):
            slot = 2 * k + q
            one, two = ext[block + 1, slot], ext[block, slot]
            if p < 3 or q == 0:
                plane = p * LEV + 2 * e + q if p < 3 else 3 * LEV
                put(plane, rows(jnp.where(own_j >= 0, gather(one, own_i), gather(two, own_i))))
            out = jnp.where(end_j >= 0, gather(one, end_i), gather(two, end_i))
            out = jnp.where(end_j >= LANES, gather(ext[block + 2, slot], end_i), out)
            both.append(jnp.where(end_j < -LANES, gather(ext[block - 1, slot], end_i), out))
        put(PLANES + k, rows(pair_up(both[0], both[1], shape)))


def band_kernel(mirror, edge, hedge, scale, body, fa, fb, *rest):
    lats, (out_ref, one, two, xb, yb, rb, coef, ext, res, sem) = rest[:-10], rest[-10:]
    inner_rows = pl.ds(SUB, body.shape[1] - 2 * SUB)
    copies = [pltpu.make_async_copy(body.at[:, inner_rows, :], out_ref.at[:, inner_rows, :], sem.at[2])]
    copies[0].start()
    side = edge.shape[1] // 2
    count = LEV + EDGES
    even = is_even("lon")
    lat_even = is_even("lat")
    is_top = lax.axis_index("lat") == lax.axis_size("lat") - 1
    lo = SUB
    north, south, own = lo + side, lo + side + SUB, lo + side + 2 * SUB
    hi = own + side
    clear_pads((one, two, xb, yb), count, lo, hi)

    def ghost(plane, of_even, of_odd):
        from_even, from_odd = [lats[i][plane] if i < len(lats) else jnp.zeros((SUB, LANES), F32) for i in (of_even, of_odd)]
        return jnp.where(lat_even, from_even, from_odd)

    def place(plane):
        if plane < 3 * LEV:
            return (one, xb, yb)[plane // LEV].at[plane % LEV]
        if plane == 3 * LEV:
            return rb.at[0]
        p, e = divmod(plane - PLANES, EDGES)
        return rb.at[1] if p == 3 else (one, xb, yb)[p].at[LEV + e]

    for plane in range(ALL):
        ref = place(plane)
        mine = edge.at[plane] if plane < PLANES else hedge.at[plane - PLANES]
        ref[pl.ds(lo, side), :] = mine[:side, :]
        ref[pl.ds(own, side), :] = mine[side:, :]
        ref[pl.ds(south, SUB), :] = ghost(plane, 1, 0)

    @pl.when(is_top)
    def _():
        def put(plane, value):
            place(plane)[pl.ds(north, SUB), :] = value

        def near(at):
            return jnp.where(even, fa[pl.ds(at, SUB), :], fb[pl.ds(at, SUB), :])

        def far(at):
            return jnp.where(even, fb[pl.ds(at, SUB), :], fa[pl.ds(at, SUB), :])

        center = jnp.max(mirror[...].reshape(1, LANES))
        mirrored(near, far, fa.shape[0] > 2 * TOP, center, ext, put)

    @pl.when(jnp.logical_not(is_top))
    def _():
        for plane in range(ALL):
            place(plane)[pl.ds(north, SUB), :] = ghost(plane, 0, 1)

    n = hi - lo
    row = lo + lax.broadcasted_iota(jnp.int32, (n, LANES), 0)
    fold = is_top & (row >= north) & (row < south)
    n_far = jnp.where(is_top & (row == north - 1), 0.5, jnp.where(fold, 1.0, 0.0))
    s_far = jnp.where(is_top & (row == north), 0.5, jnp.where(fold, 1.0, 0.0))
    weights = (fold, 1.0 - n_far, n_far, 1.0 - s_far, s_far)
    for c in range(count):
        coefficients(xb, yb, rb[c // LEV, pl.ds(lo, n), :], c, lo, n, coef, weights)
    run_steps(one, two, coef, count, lo, hi, n)
    for l in range(LEV):
        for i, at in enumerate((north - SUB, own)):
            rows = pl.ds(at, SUB)
            value = merge(one[l, rows, :], one[LEV + l // 2, rows, :], l)
            res[i, l] = scale[l, i * SUB : (i + 1) * SUB, :] * value
    rows = out_ref.shape[1]
    copies += [
        pltpu.make_async_copy(res.at[0], out_ref.at[:, pl.ds(rows - SUB, SUB), :], sem.at[0]),
        pltpu.make_async_copy(res.at[1], out_ref.at[:, pl.ds(0, SUB), :], sem.at[1]),
    ]
    for copy in copies[1:]:
        copy.start()
    for copy in copies:
        copy.wait()


def band(mirror, edge, hedge, scale, body, fa, fb, lats):
    vm = pl.BlockSpec(memory_space=pltpu.VMEM)
    anywhere = pl.BlockSpec(memory_space=pl.ANY)
    pad = edge.shape[1] + 4 * SUB
    cells = pltpu.VMEM((LEV + EDGES, pad, LANES), F32)
    return pl.pallas_call(
        band_kernel,
        in_specs=[vm] * (7 + len(lats)),
        out_specs=anywhere,
        out_shape=pltpu.HBM(body.shape, F32),
        scratch_shapes=[
            cells,
            cells,
            cells,
            cells,
            pltpu.VMEM((2, pad, LANES), F32),
            pltpu.VMEM((5, LEV + EDGES, pad, LANES), F32),
            pltpu.VMEM((6, 2 * ENDS, SUB, LANES), F32),
            pltpu.VMEM((2, LEV, SUB, LANES), F32),
            pltpu.SemaphoreType.DMA((3,)),
        ],
        compiler_params=pltpu.CompilerParams(vmem_limit_bytes=VMEM_LIMIT),
        name="band",
    )(mirror, edge, hedge, scale, body, fa, fb, *lats)


def table(axes, sizes, send):
    place = {axis: i for i, axis in enumerate(axes)}

    def flat(lon, lat):
        spot = {"lon": lon, "lat": lat}
        index = 0
        for axis in axes:
            index = index * sizes[axis] + spot[axis]
        return index

    pairs = []
    for lon in range(sizes["lon"]):
        for lat in range(sizes["lat"]):
            to = send(lon, lat)
            if to is not None:
                pairs.append((flat(lon, lat), flat(to[0] % sizes["lon"], to[1])))
    return pairs


def per_device(axes, sizes, inc, kx, ky, mx, my, area, mask, fold_partner, norm):
    n_lon, n_lat = sizes["lon"], sizes["lat"]
    chips = n_lon // 2

    def permute(x, send):
        return lax.ppermute(x, axes, table(axes, sizes, send))

    def sibling(o, a):
        return o + 1 - 2 * (o % 2), a

    def outer(o, a):
        return o - 1 + 2 * (o % 2), a

    def even_lat(o, a):
        return o, a + 1 - 2 * (a % 2)

    def odd_lat(o, a):
        to = a - 1 + 2 * (a % 2)
        return (o, to) if 0 <= to < n_lat else None

    def across(chip):
        def send(o, a):
            if a < n_lat - 1:
                return sibling(o, a)
            return (2 * ((chip - o // 2) % chips), a) if o % 2 else (2 * ((chip - 1 - o // 2) % chips) + 1, a)

        return lambda x: permute(x, send)

    def finish(over_fold):
        def branch(m0, m1, edge, chip, mirror, fields, norm):
            g0 = permute(m0, sibling)
            g1 = permute(m1, outer)
            fold = join(m0, g0)
            if over_fold is not None:
                fa = over_fold(fold)
                fold, fields = lax.optimization_barrier((fold, fields))
            mid, ends = inner(*fields)
            edge, mid = lax.optimization_barrier((edge, mid))
            hedge, *rows = edge_messages(g0, g1, edge, 1 if n_lat == 2 else 2)
            if over_fold is None:
                fa = lax.switch(chip[0], [across(i) for i in range(chips)], join_ends(fold, hedge))
            lats = [permute(x, send) for x, send in zip(rows, (even_lat, odd_lat))]
            body, scale = lon_ends(ends, g0, g1, mid, norm, fields[5])
            fa, scale = lax.optimization_barrier((fa, scale))
            fb = permute(fa, sibling)
            return band(mirror, edge, hedge, scale, body, fa, fb, lats)

        return branch

    fields = (inc, kx, ky, mx, my, area, mask)
    edge, m0, m1, way, chip, mirror = pack(lead(), fold_partner, *fields)
    branches = [finish(across(i)) for i in range(chips)] + [finish(None)]
    return lax.switch(way[0], branches, m0, m1, edge, chip, mirror, fields, norm)


def solution(mesh):
    axes = tuple(mesh.axis_names)
    sizes = dict(mesh.shape)
    cube, flat = P(None, "lat", "lon"), P("lat", "lon")
    return jax.shard_map(
        functools.partial(per_device, axes, sizes),
        mesh=mesh,
        in_specs=(cube, cube, cube, flat, flat, flat, cube, P("lon"), cube),
        out_specs=cube,
        check_vma=False,
    )
```
